512 devices in a mesh: seg: 64 (over x, z), grp: 4 (over y), pair: 2 (over core).
Axes of the slice: x: 4, y: 4, z: 16, core: 2. Of those that a mesh axis runs over, the one named last changes fastest.
Arguments:
- observations: float32 [2048, 256], P(('grp', 'seg')), may hold values from -6 to 6
- masks: int32 [2048, 256], P(('grp', 'seg')), may hold values 0 or 1
- gains: float32 [256], replicated, may hold values from 0.05 to 0.5
- transition: float32 [256, 256], replicated, may hold values from -1 to 1, as said below
- smoother_scale: float32 [256], replicated, may hold values from 0.995 to 0.9999
- initial_mean: float32 [256], replicated, may hold values from -8 to 8
Outputs:
- filtered: float32 [2048, 256], P(('grp', 'seg'), 'pair')
- smoothed: float32 [2048, 256], P(('grp', 'seg'), 'pair')
The draws below stay inside these ranges and needn't reach their ends.
Inputs may be any that keep to these rules, and one draw needn't show every extreme that they name: Each column of transition is a unit vector scaled by a factor in (0, 1); the columns are orthogonal.
All inputs are finite; a program needn't handle non-finite values. No bound on the sum of `masks` on one device may be relied on, other than what follows from the above.
Results may differ from the reference program's by a relative error of at most 0.0003.
Values sent between devices are 32-bit elements; how exact they have to be, the bound alone decides.
A program may use at most 64 MiB of HBM per device.

```python
import math
import jax
import jax.numpy as jnp
from jax import lax

M = 256
DAYS = 2048


def draw_transition(key, part):
    key_basis, key_share, key_fast = jax.random.split(jax.random.fold_in(key, 11), 3)
    normals = jax.random.normal(key_basis, (M, M), jnp.float32)
    basis, upper = jnp.linalg.qr(normals)
    share = 0.5
    picks = jax.random.uniform(key_share, (M,), jnp.float32)
    slow_rate = jnp.exp(jnp.log(0.2) / DAYS)
    fast_rate = jnp.exp(-1.0 / jax.random.uniform(key_fast, (M,), jnp.float32, 30.0, 50.0))
    rates = jnp.where(picks < share, slow_rate, fast_rate)
    return (basis * rates[None, :]).astype(jnp.float32)


def with_ends(result, own_key, least, high):
    spot = [jax.random.randint(jax.random.fold_in(own_key, axis), (), 0, length) for axis, length in enumerate(result.shape)]
    main_axis = result.shape.index(max(result.shape))
    beside = spot[:main_axis] + [(spot[main_axis] + 1) % result.shape[main_axis]] + spot[main_axis + 1:]
    return result.at[tuple(spot)].set(least).at[tuple(beside)].set(high)


def block_scale(stream_key, shape, cuts, smallest, high):
    def one(dim, blocks):
        steps = jax.random.uniform(jax.random.fold_in(jax.random.fold_in(stream_key, 6), dim), (blocks,), jnp.float32, smallest / len(cuts), high / len(cuts))
        return jnp.repeat(jnp.exp(steps), shape[dim] // blocks).reshape((-1,) + (1,) * (len(shape) - dim - 1))

    factor_of = one(*cuts[0])
    for cut in cuts[1:]:
        factor_of = factor_of * one(*cut)
    return factor_of


def centred(own_key, dims, width, most, cuts=(), kind=jnp.bfloat16):
    array = width * jax.random.normal(own_key, dims, jnp.float32)
    if cuts:
        array = array * block_scale(own_key, dims, cuts, -0.22, 0.18)
    return jnp.clip(array, -most, most).astype(kind)


def setup_inputs(seed: int = 0) -> dict:
    seeds = jax.random.split(jax.random.key(seed), 7)
    observations = centred(seeds[0], (DAYS, M), 1.0, 6.0, ((0, 256),), jnp.float32)
    masks = with_ends((jax.random.randint(seeds[1], (DAYS, M), 0, 32) < 1).astype(jnp.int32), jax.random.fold_in(seeds[1], 1), 0, 1)
    gains = jnp.clip(jnp.exp(jax.random.uniform(seeds[2], (M,), jnp.float32, math.log(0.05), math.log(0.5))), 0.05, 0.5)
    transition = draw_transition(jax.random.fold_in(seeds[6], 71), 0)
    smoother_scale = jnp.clip(jnp.exp(jax.random.uniform(seeds[4], (M,), jnp.float32, math.log(0.995), math.log(0.9999))), 0.995, 0.9999)
    initial_mean = centred(seeds[5], (M,), 2.0, 8.0, (), jnp.float32)
    return dict(observations=observations, masks=masks, gains=gains, transition=transition, smoother_scale=smoother_scale, initial_mean=initial_mean)


def reference(observations, masks, gains, transition, smoother_scale, initial_mean):
    highest = lax.Precision.HIGHEST
    observed = masks.astype(jnp.float32) * gains[None, :]
    retain = 1.0 - observed
    forcing = observed * observations
    smoother_gain = smoother_scale[:, None] * transition.T

    def forward_step(mean_prev, row_pair):
        retain_row, forcing_row = row_pair
        mean_next = retain_row * jnp.dot(transition, mean_prev, precision=highest) + forcing_row
        return (mean_next, mean_next)
    unused, filtered = lax.scan(forward_step, initial_mean, (retain, forcing))
    boundary = jnp.dot(transition, filtered[-1], precision=highest)

    def backward_step(smooth_next, mean_here):
        predicted = jnp.dot(transition, mean_here, precision=highest)
        smooth_here = mean_here + jnp.dot(smoother_gain, smooth_next - predicted, precision=highest)
        return (smooth_here, smooth_here)
    unused_two, smoothed = lax.scan(backward_step, boundary, filtered, reverse=True)
    return (filtered, smoothed)
```

```python
import jax
import jax.numpy as jnp
from jax import lax
from jax.experimental import pallas as pl
from jax.experimental.pallas import tpu as pltpu
from jax.sharding import PartitionSpec as P

F32 = jnp.float32
BF16 = jnp.bfloat16
M = 256
HALF = 128
DAYS = 8
XN, YN, ZN = 4, 4, 16
QN = 4
CH = 4
QD = CH * DAYS
RD = QN * QD
POWERS = 11
NROWS = HALF + 8


def split(v):
    hi = v.astype(BF16)
    return hi, (v - hi.astype(F32)).astype(BF16)


def mm(v, whi, wlo):
    rows = v.shape[0]
    hi, lo = split(v)
    both = jnp.dot(jnp.concatenate([hi, lo], 0), whi, preferred_element_type=F32)
    return both[:rows] + both[rows:] + jnp.dot(hi, wlo, preferred_element_type=F32)


def kernel(
    obs, mask, gain, trans, scale, init, filt_out, smooth_out,
    rf, athi, atlo, hp, hphi, hplo, xk, khi, klo, nb, nhi, nlo, ret4, frc4, kap,
    gin, gout, ent, fs, fb, sb, wb, vb, eb, fh, sh, frecv, srecv,
    m_send, m_recv, r_send, r_recv, k_send, k_recv, ks_send, ks_recv,
    n_send, n_recv, ns_send, ns_recv, g_send, g_recv, v_send, v_recv,
    of_send, os_send, of_recv, os_recv,
):
    seg, y, c = lax.axis_index("seg"), lax.axis_index("grp"), lax.axis_index("pair")
    x, z = lax.div(seg, ZN), lax.rem(seg, ZN)
    q, r = lax.div(z, CH), lax.rem(z, CH)
    other = 1 - c

    def at(xx, yy, zz, cc):
        return {"seg": xx * ZN + zz, "grp": yy, "pair": cc}

    def copy(src, dst, send, recv, where):
        return pltpu.make_async_remote_copy(
            src_ref=src, dst_ref=dst, send_sem=send, recv_sem=recv,
            device_id=where, device_id_type=pl.DeviceIdType.MESH,
        )

    is_master, is_worker = z == 0, r == 0
    barrier = pltpu.get_barrier_semaphore()

    def greet(where):
        pl.semaphore_signal(
            barrier, inc=1, device_id=where, device_id_type=pl.DeviceIdType.MESH
        )

    @pl.when(is_worker)
    def _():
        for k in range(1, CH):
            greet(at(x, y, z + k, c))

    @pl.when(is_master)
    def _():
        for k in range(1, QN):
            greet(at(x, y, k * CH, c))
        for k in range(1, XN * YN):
            greet(at(lax.rem(x + k % XN, XN), lax.rem(y + k // XN, YN), 0, c))
        greet(at(x, y, 0, other))

    @pl.when(jnp.logical_not(is_master))
    def _():
        greet(at(x, y, 0, c))

    observed = mask[...].astype(F32) * gain[...]
    rf[z, 0:DAYS, :] = 1.0 - observed
    rf[z, DAYS : 2 * DAYS, :] = observed * obs[...]

    @pl.when(jnp.logical_not(is_worker))
    def _():
        pl.semaphore_wait(barrier, 1)
        to_worker = copy(
            rf.at[z], rf.at[z], m_send, m_recv.at[r], at(x, y, q * CH, c)
        )
        to_worker.start()
        to_worker.wait_send()

    @pl.when(is_worker)
    def _():
        at_full = trans[...].T
        ahi, alo = split(at_full)
        athi[...] = ahi
        atlo[...] = alo
        xk[q, c] = trans[...].T[0:HALF]

        @pl.when(c == 1)
        def _():
            xk[q, c] = trans[...].T[HALF:M]

        def advance(chip, first):
            def day(j, rows):
                return mm(rows, athi[...], atlo[...]) * rf[z + chip, pl.ds(j, 1), :]

            return lax.fori_loop(first, DAYS, day, xk[q, c])

        xk[q, c] = xk[q, c] * rf[z, 0:1, :]
        xk[q, c] = advance(0, 1)
        for k in range(1, CH):
            copy(
                rf.at[z + k], rf.at[z + k], m_send, m_recv.at[k], at(x, y, 0, other)
            ).wait_recv()
            xk[q, c] = advance(k, 0)

    @pl.when(jnp.logical_and(is_worker, jnp.logical_not(is_master)))
    def _():
        pl.semaphore_wait(barrier, 1)
        days_to = copy(
            rf.at[pl.ds(z, CH)], rf.at[pl.ds(z, CH)], r_send, r_recv.at[q], at(x, y, 0, c)
        )
        days_to.start()
        map_to = copy(xk.at[q, c], xk.at[q, c], k_send, k_recv.at[q], at(x, y, 0, c))
        map_to.start()
        days_to.wait_send()
        map_to.wait_send()

    @pl.when(is_master)
    def _():
        pl.semaphore_wait(barrier, ZN - 1 + XN * YN - 1 + 1)

        def to_sibling(qq):
            return copy(
                xk.at[qq, c], xk.at[qq, c], ks_send.at[qq], ks_recv.at[qq], at(x, y, 0, other)
            )

        to_sibling(0).start()

        h0 = trans[...] * scale[...]
        hp[...] = h0
        hphi[0], hplo[0] = split(h0)

        def square(k, _):
            h = hp[...]
            h = jnp.dot(h, h, precision=lax.Precision.HIGHEST, preferred_element_type=F32)
            hp[...] = h
            hphi[k], hplo[k] = split(h)
            return 0

        lax.fori_loop(1, POWERS, square, 0)

        for k in range(1, QN):
            copy(
                rf.at[pl.ds(k * CH, CH)], rf.at[pl.ds(k * CH, CH)], r_send, r_recv.at[k],
                at(x, y, 0, other),
            ).wait_recv()
        ret4[...] = jnp.zeros_like(ret4)
        frc4[...] = jnp.zeros_like(frc4)

        for qq in range(QN):
            for k in range(CH):
                ret4[k * DAYS : (k + 1) * DAYS, qq, :] = rf[qq * CH + k, 0:DAYS, :]
                frc4[k * DAYS : (k + 1) * DAYS, qq, :] = rf[qq * CH + k, DAYS : 2 * DAYS, :]

        def day4(j, rows):
            return mm(rows, athi[...], atlo[...]) * ret4[j] + frc4[j]

        kap[...] = lax.fori_loop(0, QD, day4, jnp.zeros((8, M), F32))

        for k in range(1, QN):
            copy(
                xk.at[k, c], xk.at[k, c], k_send, k_recv.at[k], at(x, y, 0, other)
            ).wait_recv()
            to_sibling(k).start()
        rows = jnp.concatenate(
            [xk[0, c], jnp.broadcast_to(kap[0:1, :], (8, M))], 0
        )
        sub = lax.broadcasted_iota(jnp.int32, (NROWS, M), 0)
        for k in range(QN):
            to_sibling(k).wait_recv()
            for half in range(2):
                khi[k, half * HALF : (half + 1) * HALF, :], klo[
                    k, half * HALF : (half + 1) * HALF, :
                ] = split(xk[k, half])
            if k:
                rows = mm(rows, khi[k], klo[k]) + jnp.where(sub < HALF, 0.0, kap[k : k + 1, :])
        nb[x, c] = rows

        def to_peer(d):
            return copy(
                nb.at[x, c], nb.at[x, c], n_send.at[d], n_recv.at[x],
                at(lax.rem(x + d, XN), y, 0, c),
            )

        def share(xs):
            return copy(
                nb.at[xs, c], nb.at[xs, c], ns_send.at[xs], ns_recv.at[xs], at(x, y, 0, other)
            )

        for d in (2, 1, 3):
            to_peer(d).start()
        share(x).start()
        for d in (1, 3, 2):
            xs = lax.rem(x + d, XN)
            copy(
                nb.at[xs, c], nb.at[xs, c], n_send.at[d], n_recv.at[xs], at(x, y, 0, other)
            ).wait_recv()
            share(xs).start()
        for xs in range(XN):
            share(xs).wait_recv()
            for half in range(2):
                nhi[xs, half * HALF : (half + 1) * HALF, :], nlo[
                    xs, half * HALF : (half + 1) * HALF, :
                ] = split(nb[xs, half, 0:HALF, :])

        @pl.when(y == 0)
        def _():
            gin[...] = jnp.broadcast_to(init[...], (8, M))

        @pl.when(y > 0)
        def _():
            copy(gin, gin, g_send, g_recv, at(x, y, 0, other)).wait_recv()

        state = gin[...]
        for k in range(XN):
            ent[k] = state
            state = mm(state, nhi[k], nlo[k]) + nb[k, 0, HALF : HALF + 1, :]
        gout[...] = state

        def to_group():
            return copy(gout, gin, g_send, g_recv, at(x, lax.rem(y + 1, YN), 0, c))

        @pl.when(y < YN - 1)
        def _():
            to_group().start()

        state = ent[x]
        fs[...] = jnp.zeros_like(fs)
        for k in range(QN):
            fs[k : k + 1, :] = state[0:1, :]
            if k < QN - 1:
                state = mm(state, khi[k], klo[k]) + kap[k : k + 1, :]

        def run4(j, rows):
            rows = day4(j, rows)
            for k in range(QN):
                fb[pl.ds(k * QD + j, 1), :] = rows[k : k + 1, :]
            return rows

        last = lax.fori_loop(0, QD, run4, fs[...])

        def out_copy(src, dst, send, recv, k):
            zz = k
            return copy(src.at[pl.ds(zz * DAYS, DAYS)], dst, send.at[k], recv, at(x, y, zz, c))

        @pl.when(c == 0)
        def _():
            fh[...] = fb[:, 0:HALF]

        @pl.when(c == 1)
        def _():
            fh[...] = fb[:, HALF:M]

        order = (8, 7, 9, 6, 10, 5, 11, 4, 12, 3, 13, 2, 14, 1, 15)
        for k in order:
            out_copy(fh, frecv, of_send, of_recv, k).start()
        filt_out[...] = fh[0:DAYS, :]

        weight = 1.0 - scale[...] * jnp.sum(trans[...] * trans[...], axis=0, keepdims=True)
        sb[0:RD, :] = fb[...] * weight
        sb[RD : RD + HALF // 2, :] = jnp.zeros((HALF // 2, M), F32)
        for k in range(7):
            sb[0:RD, :] = sb[0:RD, :] + mm(sb[1 << k : (1 << k) + RD, :], hphi[k], hplo[k])
        me = y * XN + x
        boundary = mm(jnp.broadcast_to(last[QN - 1 : QN, :], (8, M)), athi[...], atlo[...])
        sub8 = lax.broadcasted_iota(jnp.int32, (8, M), 0)
        vb[me] = jnp.where(sub8 == 0, sb[0:1, :], boundary)

        def to_plane(k):
            return copy(
                vb.at[me], vb.at[me], v_send.at[k], v_recv.at[me],
                at(lax.rem(x + k % XN, XN), lax.rem(y + k // XN, YN), 0, c),
            )

        plane = (10, 2, 8, 6, 9, 11, 14, 5, 7, 13, 15, 1, 3, 4, 12)
        for k in plane:
            to_plane(k).start()
        for k in plane:
            src = lax.rem(y + k // XN, YN) * XN + lax.rem(x + k % XN, XN)
            copy(
                vb.at[src], vb.at[src], v_send.at[k], v_recv.at[src], at(x, y, 0, other)
            ).wait_recv()

        eb[...] = jnp.zeros_like(eb)
        for k in range(1, XN * YN):
            eb[k - 1 : k, :] = vb[k, 0:1, :]
        eb[XN * YN - 1 : XN * YN, :] = vb[XN * YN - 1, 1:2, :]
        for k in range(4):
            eb[0:16, :] = eb[0:16, :] + mm(eb[1 << k : (1 << k) + 16, :], hphi[7 + k], hplo[7 + k])

        wb[RD - 8 : RD, :] = jnp.zeros((8, M), F32)
        wb[RD - 1 : RD, :] = mm(jnp.broadcast_to(eb[pl.ds(me, 1), :], (8, M)), hphi[0], hplo[0])[0:1, :]
        for k in range(7):
            n = 1 << k
            wb[RD - 2 * n : RD - n, :] = mm(
                wb[RD - max(n, 8) : RD, :], hphi[k], hplo[k]
            )[max(n, 8) - n : max(n, 8), :]
        total = sb[0:RD, :] + wb[...]

        @pl.when(c == 0)
        def _():
            sh[...] = total[:, 0:HALF]

        @pl.when(c == 1)
        def _():
            sh[...] = total[:, HALF:M]

        for k in order:
            out_copy(sh, srecv, os_send, os_recv, k).start()
        smooth_out[...] = sh[0:DAYS, :]

        for k in range(QN):
            to_sibling(k).wait_send()
        for d in range(1, XN):
            to_peer(d).wait_send()
        for xs in range(XN):
            share(xs).wait_send()

        @pl.when(y < YN - 1)
        def _():
            to_group().wait_send()

        for k in plane:
            to_plane(k).wait_send()
        for k in order:
            out_copy(fh, frecv, of_send, of_recv, k).wait_send()
            out_copy(sh, srecv, os_send, os_recv, k).wait_send()

    @pl.when(jnp.logical_not(is_master))
    def _():
        copy(frecv, frecv, r_send, of_recv, at(x, y, 0, c)).wait_recv()
        filt_out[...] = frecv[...]
        copy(srecv, srecv, r_send, os_recv, at(x, y, 0, c)).wait_recv()
        smooth_out[...] = srecv[...]


def shards(observations, masks, gains, transition, smoother_scale, initial_mean):
    vmem = pl.BlockSpec(memory_space=pltpu.VMEM)
    dma = pltpu.SemaphoreType.DMA

    def buf(*shape, dtype=F32):
        return pltpu.VMEM(shape, dtype)

    out = jax.ShapeDtypeStruct((DAYS, HALF), F32)
    return pl.pallas_call(
        kernel,
        out_shape=(out, out),
        in_specs=[vmem] * 6,
        out_specs=(vmem, vmem),
        scratch_shapes=[
            buf(ZN, 2 * DAYS, M),
            buf(M, M, dtype=BF16), buf(M, M, dtype=BF16),
            buf(M, M), buf(POWERS, M, M, dtype=BF16), buf(POWERS, M, M, dtype=BF16),
            buf(QN, 2, HALF, M), buf(QN, M, M, dtype=BF16), buf(QN, M, M, dtype=BF16),
            buf(XN, 2, NROWS, M), buf(XN, M, M, dtype=BF16), buf(XN, M, M, dtype=BF16),
            buf(QD, 8, M), buf(QD, 8, M), buf(8, M),
            buf(8, M), buf(8, M), buf(XN, 8, M),
            buf(8, M), buf(RD, M), buf(RD + HALF // 2, M), buf(RD, M),
            buf(XN * YN, 8, M), buf(32, M),
            buf(RD, HALF), buf(RD, HALF), buf(DAYS, HALF), buf(DAYS, HALF),
            dma, dma((CH,)), dma, dma((QN,)), dma, dma((QN,)), dma((QN,)), dma((QN,)),
            dma((XN,)), dma((XN,)), dma((XN,)), dma((XN,)), dma, dma,
            dma((XN * YN,)), dma((XN * YN,)),
            dma((ZN,)), dma((ZN,)), dma, dma,
        ],
        compiler_params=pltpu.CompilerParams(
            collective_id=0, has_side_effects=True, vmem_limit_bytes=48 * 2**20
        ),
        name="smoother",
    )(
        observations, masks, gains.reshape(1, M), transition,
        smoother_scale.reshape(1, M), initial_mean.reshape(1, M),
    )


def solution(mesh):
    return jax.shard_map(
        shards,
        mesh=mesh,
        in_specs=(P(("grp", "seg"), None), P(("grp", "seg"), None), P(), P(), P(), P()),
        out_specs=(P(("grp", "seg"), "pair"), P(("grp", "seg"), "pair")),
        check_vma=False,
    )
```

```python
import jax
import jax.numpy as jnp
from jax import lax
from jax.experimental import pallas as pl
from jax.experimental.pallas import tpu as pltpu
from jax.sharding import PartitionSpec as P

F32 = jnp.float32
BF16 = jnp.bfloat16
M = 256
HALF = 128
DAYS = 8
XN, YN, ZN = 4, 4, 16
QN = 4
CH = 4
QD = CH * DAYS
RINGS = XN * YN
POWERS = 11
ROWS = HALF + 8


def split(v):
    hi = v.astype(BF16)
    return hi, (v - hi.astype(F32)).astype(BF16)


def mm(v, whi, wlo):
    rows = v.shape[0]
    if rows % 16 == 8 and rows > 8:
        return jnp.concatenate([mm(v[: rows - 8], whi, wlo), mm(v[rows - 8 :], whi, wlo)], 0)
    hi, lo = split(v)
    both = jnp.dot(jnp.concatenate([hi, lo], 0), whi, preferred_element_type=F32)
    return both[:rows] + both[rows:] + jnp.dot(hi, wlo, preferred_element_type=F32)


def plus_offset(rows, offset):
    n = rows.shape[0] - rows.shape[0] % HALF
    return jnp.concatenate([rows[:n], rows[n:] + offset], 0)


def whole(halves):
    return jnp.concatenate([halves[0, 0:HALF, :], halves[1, 0:HALF, :], halves[0, HALF:ROWS, :]], 0)


def kernel(
    obs_hbm, mask_hbm, gain_hbm, trans_hbm, scale_hbm, init_hbm, filt_out, smooth_out,
    obs, mask, gain, trans, scale, init,
    rf, atf, athi, atlo, hp, hphi, hplo, xt, mk, khi, klo, mv, vo, vhi, vlo, sm, tm, pre, thi, tlo, pc, phi, plo,
    nb, nhi, nlo, ret4, frc4, gin, gout, ent, st, fs, fb, sb, wb, vb, eb,
    fh, sh, frecv, srecv,
    in_sem, m_send, m_recv, k_send, k_recv, ks_send, ks_recv, w_send, w_recv, ws_send, ws_recv,
    p_send, p_recv, n_send, n_recv, ns_send, ns_recv, g_send, g_recv, v_send, v_recv,
    of_send, os_send, of_recv, os_recv,
):
    seg, y, c = lax.axis_index("seg"), lax.axis_index("grp"), lax.axis_index("pair")
    x, z = lax.div(seg, ZN), lax.rem(seg, ZN)
    q, r = lax.div(z, CH), lax.rem(z, CH)
    other = 1 - c
    is_worker = r == 0

    fetches = [
        pltpu.make_async_copy(src, dst, in_sem.at[k])
        for k, (src, dst) in enumerate(
            (
                (mask_hbm, mask), (obs_hbm, obs), (gain_hbm, gain),
                (trans_hbm, trans), (scale_hbm, scale), (init_hbm, init),
            )
        )
    ]
    for fetch in fetches:
        fetch.start()

    def at(xx, yy, zz, cc):
        return {"seg": xx * ZN + zz, "grp": yy, "pair": cc}

    sibling = at(x, y, z, other)

    def copy(src, dst, send, recv, where):
        return pltpu.make_async_remote_copy(
            src_ref=src, dst_ref=dst, send_sem=send, recv_sem=recv,
            device_id=where, device_id_type=pl.DeviceIdType.MESH,
        )

    def arrival(dst, send, recv):
        return copy(dst, dst, send, recv, sibling)

    barrier = pltpu.get_barrier_semaphore()

    def greet(where):
        pl.semaphore_signal(
            barrier, inc=1, device_id=where, device_id_type=pl.DeviceIdType.MESH
        )

    def ring_peer(d):
        return at(x, y, lax.rem(q + d, QN) * CH, c)

    def plane_peer(k):
        return at(lax.rem(x + k % XN, XN), lax.rem(y + k // XN, YN), z, c)

    @pl.when(is_worker)
    def _():
        for k in range(1, CH):
            greet(at(x, y, z + k, c))
        for k in range(1, QN):
            greet(ring_peer(k))
        for k in range(1, RINGS):
            greet(plane_peer(k))
        greet(sibling)

    @pl.when(jnp.logical_not(is_worker))
    def _():
        greet(at(x, y, q * CH, c))

    for fetch in fetches[:3]:
        fetch.wait()
    observed = mask[...].astype(F32) * gain[...]
    rf[r, 0:DAYS, :] = 1.0 - observed
    rf[r, DAYS : 2 * DAYS, :] = observed * obs[...]

    @pl.when(jnp.logical_not(is_worker))
    def _():
        pl.semaphore_wait(barrier, 1)
        to_worker = copy(rf.at[r], rf.at[r], m_send, m_recv.at[r], at(x, y, q * CH, c))
        to_worker.start()
        for fetch in fetches[3:]:
            fetch.wait()
        to_worker.wait_send()
        arrival(frecv, m_send, of_recv).wait_recv()
        filt_out[...] = frecv[...]
        arrival(srecv, m_send, os_recv).wait_recv()
        smooth_out[...] = srecv[...]

    @pl.when(is_worker)
    def _():
        for fetch in fetches[3:]:
            fetch.wait()

        at_full = trans[...].T
        atf[...] = at_full
        athi[...], atlo[...] = split(at_full)
        h0 = trans[...] * scale[...]
        hp[...] = h0
        hphi[0], hplo[0] = split(h0)

        def advance(chip, first, rows):
            def day(j, rows):
                rows = plus_offset(
                    mm(rows, athi[...], atlo[...]) * rf[chip, pl.ds(j, 1), :],
                    rf[chip, pl.ds(DAYS + j, 1), :],
                )
                xt[chip * DAYS + j] = rows
                return rows

            return lax.fori_loop(first, DAYS, day, rows)

        rows = jnp.concatenate(
            [
                atf[pl.ds(pl.multiple_of(c * HALF, HALF), HALF), :] * rf[0, 0:1, :],
                jnp.broadcast_to(rf[0, DAYS : DAYS + 1, :], (8, M)),
            ],
            0,
        )
        xt[0] = rows
        rows = advance(0, 1, rows)
        for k in range(1, CH):
            arrival(rf.at[k], m_send, m_recv.at[k]).wait_recv()
            rows = advance(k, 0, rows)
        mk[q, c] = rows

        pl.semaphore_wait(barrier, CH - 1 + QN - 1 + RINGS - 1 + 1)

        def ring_send(buf, send, recv, d):
            return copy(buf.at[q, c], buf.at[q, c], send.at[d], recv.at[q], ring_peer(d))

        def ring_share(buf, send, recv, k):
            return copy(buf.at[k, c], buf.at[k, c], send.at[k], recv.at[k], sibling)

        for d in (2, 1, 3):
            ring_send(mk, k_send, k_recv, d).start()
        ring_share(mk, ks_send, ks_recv, q).start()

        def chunk_share(k):
            return copy(xt.at[k * DAYS - 1], pc.at[k - 1], p_send.at[k - 1], p_recv.at[k - 1], sibling)

        for k in range(1, CH):
            chunk_share(k).start()

        weight = 1.0 - scale[...] * jnp.sum(trans[...] * trans[...], axis=0, keepdims=True)

        def back(k, rows):
            return xt[QD - 2 - k] * weight + mm(rows, hphi[0], hplo[0])

        mv[q, c] = lax.fori_loop(0, QD - 1, back, xt[QD - 1] * weight)

        for d in (1, 3, 2):
            k = lax.rem(q + d, QN)
            arrival(mk.at[k, c], k_send.at[d], k_recv.at[k]).wait_recv()
            ring_share(mk, ks_send, ks_recv, k).start()
        for d in (2, 1, 3):
            ring_send(mv, w_send, w_recv, d).start()
        ring_share(mv, ws_send, ws_recv, q).start()
        for k in range(QN):
            ring_share(mk, ks_send, ks_recv, k).wait_recv()
            for half in range(2):
                part = slice(half * HALF, (half + 1) * HALF)
                khi[k, part, :], klo[k, part, :] = split(mk[k, half, 0:HALF, :])
        rows = mk[0, c]
        for k in range(1, QN):
            rows = plus_offset(mm(rows, khi[k], klo[k]), mk[k, 0, HALF : HALF + 1, :])
        nb[x, c] = rows

        def to_peer(d):
            return copy(
                nb.at[x, c], nb.at[x, c], n_send.at[d], n_recv.at[x],
                at(lax.rem(x + d, XN), y, z, c),
            )

        def share(xs):
            return copy(nb.at[xs, c], nb.at[xs, c], ns_send.at[xs], ns_recv.at[xs], sibling)

        for d in (2, 1, 3):
            to_peer(d).start()
        share(x).start()

        def square(k, _):
            h = hp[...]
            h = jnp.dot(h, h, precision=lax.Precision.HIGHEST, preferred_element_type=F32)
            hp[...] = h
            hphi[k], hplo[k] = split(h)
            return 0

        lax.fori_loop(1, POWERS, square, 0)
        ret4[...] = jnp.zeros_like(ret4)
        frc4[...] = jnp.zeros_like(frc4)
        for k in range(CH):
            ret4[:, k, :] = rf[k, 0:DAYS, :]
            frc4[:, k, :] = rf[k, DAYS : 2 * DAYS, :]
        for k in range(1, CH):
            arrival(pc.at[k - 1], p_send.at[k - 1], p_recv.at[k - 1]).wait_recv()
            mine, theirs = split(xt[k * DAYS - 1, 0:HALF, :]), split(pc[k - 1, 0:HALF, :])
            own = pl.ds(pl.multiple_of(c * HALF, HALF), HALF)
            far = pl.ds(pl.multiple_of(other * HALF, HALF), HALF)
            phi[k - 1, own, :], plo[k - 1, own, :] = mine
            phi[k - 1, far, :], plo[k - 1, far, :] = theirs
        for d in (1, 3, 2):
            xs = lax.rem(x + d, XN)
            arrival(nb.at[xs, c], n_send.at[d], n_recv.at[xs]).wait_recv()
            share(xs).start()
        for xs in range(XN):
            share(xs).wait_recv()
            for half in range(2):
                part = slice(half * HALF, (half + 1) * HALF)
                nhi[xs, part, :], nlo[xs, part, :] = split(nb[xs, half, 0:HALF, :])

        def smoother_map():
            for d in (1, 3, 2):
                k = lax.rem(q + d, QN)
                arrival(mv.at[k, c], w_send.at[d], w_recv.at[k]).wait_recv()
                ring_share(mv, ws_send, ws_recv, k).start()
            for k in range(QN):
                ring_share(mv, ws_send, ws_recv, k).wait_recv()
            sm[...] = whole(mv[QN - 1])
            for k in (2, 1, 0):

                @pl.when(q == k)
                def _():
                    vhi[1], vlo[1] = split(sm[0:M, :])
                    vo[1] = sm[M : M + 8, :]

                later = mm(sm[...], hphi[5], hplo[5])
                lhi, llo = split(later[:M])
                sm[...] = (
                    plus_offset(mm(whole(mk[k]), lhi, llo), later[M:]) + whole(mv[k])
                )
            vhi[0], vlo[0] = split(sm[0:M, :])
            vo[0] = sm[M : M + 8, :]

        def group_map():
            tm[...] = whole(nb[0])
            for k in range(1, XN):

                @pl.when(x == k)
                def _():
                    pre[...] = tm[...]

                tm[...] = plus_offset(mm(tm[...], nhi[k], nlo[k]), nb[k, 0, HALF : HALF + 1, :])
            thi[0], tlo[0] = split(tm[0:M, :])
            thi[1], tlo[1] = split(pre[0:M, :])

        def to_group():
            return copy(gout, gin, g_send, g_recv, at(x, lax.rem(y + 1, YN), z, c))

        @pl.when(y == 0)
        def _():
            state = jnp.broadcast_to(init[...], (8, M))
            for k in range(XN):
                ent[k] = state
                state = mm(state, nhi[k], nlo[k]) + nb[k, 0, HALF : HALF + 1, :]
            gout[...] = state
            to_group().start()
            st[0] = ent[x]

        @pl.when(y > 0)
        def _():
            group_map()

        @pl.when(y > 1)
        def _():
            smoother_map()

        @pl.when(y > 0)
        def _():
            arrival(gin, g_send, g_recv).wait_recv()
            gout[...] = mm(gin[...], thi[0], tlo[0]) + tm[M : M + 1, :]

            @pl.when(y < YN - 1)
            def _():
                to_group().start()

            st[0] = jnp.where(
                x == 0, gin[...], mm(gin[...], thi[1], tlo[1]) + pre[M : M + 1, :]
            )

        @pl.when(y < 2)
        def _():
            smoother_map()

        v = (mm(st[0], vhi[0], vlo[0]) + vo[0, 0:1, :])[0:1, :]
        boundary = mm(gout[...], athi[...], atlo[...])
        me = y * XN + x
        sub8 = lax.broadcasted_iota(jnp.int32, (8, M), 0)
        vb[me] = jnp.where(sub8 == 0, v, boundary)

        def to_plane(k):
            return copy(vb.at[me], vb.at[me], v_send.at[k], v_recv.at[me], plane_peer(k))

        plane = (10, 2, 8, 6, 9, 11, 14, 5, 7, 13, 15, 1, 3, 4, 12)
        for k in plane:
            to_plane(k).start()

        for k in range(1, QN):
            st[k] = mm(st[k - 1], khi[k - 1], klo[k - 1]) + mk[k - 1, 0, HALF : HALF + 1, :]
        state = st[q]
        after = mm(st[lax.min(q + 1, QN - 1)], vhi[1], vlo[1]) + vo[1, 0:1, :]
        fs[...] = jnp.zeros_like(fs)
        fs[0:1, :] = state[0:1, :]
        for k in range(1, CH):
            fs[k : k + 1, :] = (
                mm(state, phi[k - 1], plo[k - 1]) + pc[k - 1, HALF : HALF + 1, :]
            )[0:1, :]
        days = fs[...]
        for j in range(DAYS):
            days = mm(days, athi[...], atlo[...]) * ret4[j] + frc4[j]
            for k in range(CH):
                fb[k * DAYS + j : k * DAYS + j + 1, :] = days[k : k + 1, :]

        @pl.when(c == 0)
        def _():
            fh[...] = fb[:, 0:HALF]

        @pl.when(c == 1)
        def _():
            fh[...] = fb[:, HALF:M]

        def out_copy(src, dst, send, recv, k):
            return copy(
                src.at[pl.ds(k * DAYS, DAYS)], dst, send.at[k], recv, at(x, y, z + k, c)
            )

        for k in (3, 2, 1):
            out_copy(fh, frecv, of_send, of_recv, k).start()
        filt_out[...] = fh[0:DAYS, :]

        sb[0:QD, :] = fb[...] * weight
        sb[QD : 2 * QD, :] = jnp.zeros((QD, M), F32)
        for k in range(5):
            sb[0:QD, :] = sb[0:QD, :] + mm(sb[1 << k : (1 << k) + QD, :], hphi[k], hplo[k])

        eb[...] = jnp.zeros_like(eb)
        for k in plane:
            src = lax.rem(y + k // XN, YN) * XN + lax.rem(x + k % XN, XN)
            arrival(vb.at[src], v_send.at[k], v_recv.at[src]).wait_recv()
        for k in range(1, RINGS):
            eb[k - 1 : k, :] = vb[k, 0:1, :]
        eb[RINGS - 1 : RINGS, :] = vb[RINGS - 1, 1:2, :]
        for k in range(4):
            eb[0:16, :] = eb[0:16, :] + mm(eb[1 << k : (1 << k) + 16, :], hphi[7 + k], hplo[7 + k])
        behind = jnp.broadcast_to(eb[pl.ds(me, 1), :], (8, M))
        left = QN - 1 - q
        behind = jnp.where(lax.rem(left, 2) == 1, mm(behind, hphi[5], hplo[5]), behind)
        behind = jnp.where(left >= 2, mm(behind, hphi[6], hplo[6]), behind)
        behind = jnp.where(left > 0, behind + after, behind)

        wb[QD - 8 : QD, :] = jnp.zeros((8, M), F32)
        wb[QD - 1 : QD, :] = mm(behind, hphi[0], hplo[0])[0:1, :]
        for k in range(5):
            n = 1 << k
            m = max(n, 8)
            wb[QD - 2 * n : QD - n, :] = mm(wb[QD - m : QD, :], hphi[k], hplo[k])[m - n : m, :]
        total = sb[0:QD, :] + wb[...]

        @pl.when(c == 0)
        def _():
            sh[...] = total[:, 0:HALF]

        @pl.when(c == 1)
        def _():
            sh[...] = total[:, HALF:M]

        for k in (3, 2, 1):
            out_copy(sh, srecv, os_send, os_recv, k).start()
        smooth_out[...] = sh[0:DAYS, :]

        for d in range(1, QN):
            ring_send(mk, k_send, k_recv, d).wait_send()
            ring_send(mv, w_send, w_recv, d).wait_send()
            chunk_share(d).wait_send()
        for k in range(QN):
            ring_share(mk, ks_send, ks_recv, k).wait_send()
            ring_share(mv, ws_send, ws_recv, k).wait_send()
        for d in range(1, XN):
            to_peer(d).wait_send()
        for xs in range(XN):
            share(xs).wait_send()

        @pl.when(y < YN - 1)
        def _():
            to_group().wait_send()

        for k in plane:
            to_plane(k).wait_send()
        for k in (3, 2, 1):
            out_copy(fh, frecv, of_send, of_recv, k).wait_send()
            out_copy(sh, srecv, os_send, os_recv, k).wait_send()


def shards(observations, masks, gains, transition, smoother_scale, initial_mean):
    hbm, vmem = pl.BlockSpec(memory_space=pltpu.HBM), pl.BlockSpec(memory_space=pltpu.VMEM)
    dma = pltpu.SemaphoreType.DMA

    def buf(*shape, dtype=F32):
        return pltpu.VMEM(shape, dtype)

    def halves(*shape):
        return [buf(*shape, dtype=BF16), buf(*shape, dtype=BF16)]

    out = jax.ShapeDtypeStruct((DAYS, HALF), F32)
    return pl.pallas_call(
        kernel,
        out_shape=(out, out),
        in_specs=[hbm] * 6,
        out_specs=(vmem, vmem),
        scratch_shapes=[
            buf(DAYS, M), buf(DAYS, M, dtype=jnp.int32), buf(1, M), buf(M, M), buf(1, M), buf(1, M),
            buf(CH, 2 * DAYS, M), buf(M, M), *halves(M, M),
            buf(M, M), *halves(POWERS, M, M),
            buf(QD, ROWS, M),
            buf(QN, 2, ROWS, M), *halves(QN, M, M),
            buf(QN, 2, ROWS, M), buf(2, 8, M), *halves(2, M, M),
            buf(M + 8, M), buf(M + 8, M), buf(M + 8, M), *halves(2, M, M),
            buf(CH - 1, ROWS, M), *halves(CH - 1, M, M),
            buf(XN, 2, ROWS, M), *halves(XN, M, M),
            buf(DAYS, 8, M), buf(DAYS, 8, M),
            buf(8, M), buf(8, M), buf(XN, 8, M), buf(QN, 8, M),
            buf(8, M), buf(QD, M), buf(2 * QD, M), buf(QD, M),
            buf(RINGS, 8, M), buf(32, M),
            buf(QD, HALF), buf(QD, HALF), buf(DAYS, HALF), buf(DAYS, HALF),
            dma((6,)), dma, dma((CH,)),
            dma((QN,)), dma((QN,)), dma((QN,)), dma((QN,)),
            dma((QN,)), dma((QN,)), dma((QN,)), dma((QN,)),
            dma((CH,)), dma((CH,)),
            dma((XN,)), dma((XN,)), dma((XN,)), dma((XN,)),
            dma, dma, dma((RINGS,)), dma((RINGS,)),
            dma((CH,)), dma((CH,)), dma, dma,
        ],
        compiler_params=pltpu.CompilerParams(
            collective_id=0, has_side_effects=True, vmem_limit_bytes=48 * 2**20
        ),
        name="smoother",
    )(
        observations, masks, gains.reshape(1, M), transition,
        smoother_scale.reshape(1, M), initial_mean.reshape(1, M),
    )


def solution(mesh):
    return jax.shard_map(
        shards,
        mesh=mesh,
        in_specs=(P(("grp", "seg"), None), P(("grp", "seg"), None), P(), P(), P(), P()),
        out_specs=(P(("grp", "seg"), "pair"), P(("grp", "seg"), "pair")),
        check_vma=False,
    )
```

```python
import jax
import jax.numpy as jnp
from jax import lax
from jax.experimental import pallas as pl
from jax.experimental.pallas import tpu as pltpu
from jax.sharding import PartitionSpec as P

F32 = jnp.float32
BF16 = jnp.bfloat16
M = 256
HALF = 128
DAYS = 8
XN, YN, ZN = 4, 4, 16
QN = 4
WORKER = (1, 4, 8, 12)
CH = 4
QD = CH * DAYS
RINGS = XN * YN
POWERS = 11
ROWS = HALF + 8


def split(v):
    hi = v.astype(BF16)
    return hi, (v - hi.astype(F32)).astype(BF16)


def mm(v, whi, wlo):
    rows = v.shape[0]
    if rows % 16 == 8 and rows > 8:
        return jnp.concatenate([mm(v[: rows - 8], whi, wlo), mm(v[rows - 8 :], whi, wlo)], 0)
    hi, lo = split(v)
    both = jnp.dot(jnp.concatenate([hi, lo], 0), whi, preferred_element_type=F32)
    return both[:rows] + both[rows:] + jnp.dot(hi, wlo, preferred_element_type=F32)


def plus_offset(rows, offset):
    n = rows.shape[0] - rows.shape[0] % HALF
    return jnp.concatenate([rows[:n], rows[n:] + offset], 0)


def whole(halves):
    return jnp.concatenate([halves[0, 0:HALF, :], halves[1, 0:HALF, :], halves[0, HALF:ROWS, :]], 0)


def kernel(
    obs_hbm, mask_hbm, gain_hbm, trans_hbm, scale_hbm, init_hbm, both_out,
    obs, mask, gain, trans, scale, init,
    rf, atf, athi, atlo, hp, hphi, hplo, xt, mk, khi, klo, mv, vo, vhi, vlo, sm, tm, pre, thi, tlo, pc, phi, plo,
    nb, nhi, nlo, ret4, frc4, gin, gout, ent, st, fs, fb, sb, wb, vb, eb,
    fh, sh, frecv, srecv,
    in_sem, m_send, m_recv, k_send, k_recv, ks_send, ks_recv, w_send, w_recv, ws_send, ws_recv,
    p_send, p_recv, n_send, n_recv, ns_send, ns_recv, g_send, g_recv, v_send, v_recv,
    of_send, os_send, of_recv, os_recv,
):
    seg, y, c = lax.axis_index("seg"), lax.axis_index("grp"), lax.axis_index("pair")
    x, z = lax.div(seg, ZN), lax.rem(seg, ZN)
    q, r = lax.div(z, CH), lax.rem(z, CH)
    other = 1 - c

    def place(k):
        return jnp.where(
            k < 2,
            jnp.where(k == 0, WORKER[0], WORKER[1]),
            jnp.where(k == 2, WORKER[2], WORKER[3]),
        )

    wz = place(q)
    is_worker = z == wz

    fetches = [
        pltpu.make_async_copy(src, dst, in_sem.at[k])
        for k, (src, dst) in enumerate(
            (
                (mask_hbm, mask), (obs_hbm, obs), (gain_hbm, gain),
                (trans_hbm, trans), (scale_hbm, scale), (init_hbm, init),
            )
        )
    ]
    for fetch in fetches:
        fetch.start()

    def at(xx, yy, zz, cc):
        return {"seg": xx * ZN + zz, "grp": yy, "pair": cc}

    sibling = at(x, y, z, other)

    def copy(src, dst, send, recv, where):
        return pltpu.make_async_remote_copy(
            src_ref=src, dst_ref=dst, send_sem=send, recv_sem=recv,
            device_id=where, device_id_type=pl.DeviceIdType.MESH,
        )

    def arrival(dst, send, recv):
        return copy(dst, dst, send, recv, sibling)

    barrier = pltpu.get_barrier_semaphore()

    def greet(where):
        pl.semaphore_signal(
            barrier, inc=1, device_id=where, device_id_type=pl.DeviceIdType.MESH
        )

    def ring_peer(d):
        return at(x, y, place(lax.rem(q + d, QN)), c)

    def plane_peer(k):
        return at(lax.rem(x + k % XN, XN), lax.rem(y + k // XN, YN), z, c)

    @pl.when(is_worker)
    def _():
        for k in range(1, CH):
            greet(at(x, y, q * CH + lax.rem(r + k, CH), c))
        for k in range(1, QN):
            greet(ring_peer(k))
        for k in range(1, RINGS):
            greet(plane_peer(k))
        greet(sibling)

    @pl.when(jnp.logical_not(is_worker))
    def _():
        greet(at(x, y, wz, c))

    for fetch in fetches[:3]:
        fetch.wait()
    observed = mask[...].astype(F32) * gain[...]
    rf[r, 0:DAYS, :] = 1.0 - observed
    rf[r, DAYS : 2 * DAYS, :] = observed * obs[...]

    @pl.when(jnp.logical_not(is_worker))
    def _():
        pl.semaphore_wait(barrier, 1)
        to_worker = copy(rf.at[r], rf.at[r], m_send, m_recv.at[r], at(x, y, wz, c))
        to_worker.start()
        for fetch in fetches[3:]:
            fetch.wait()
        to_worker.wait_send()
        arrival(frecv, m_send, of_recv).wait_recv()
        both_out[0:DAYS] = frecv[...]
        arrival(srecv, m_send, os_recv).wait_recv()
        both_out[DAYS:] = srecv[...]

    @pl.when(is_worker)
    def _():
        for fetch in fetches[3:]:
            fetch.wait()

        at_full = trans[...].T
        atf[...] = at_full
        athi[...], atlo[...] = split(at_full)
        h0 = trans[...] * scale[...]
        hp[...] = h0
        hphi[0], hplo[0] = split(h0)

        def advance(chip, first, rows):
            def day(j, rows):
                rows = plus_offset(
                    mm(rows, athi[...], atlo[...]) * rf[chip, pl.ds(j, 1), :],
                    rf[chip, pl.ds(DAYS + j, 1), :],
                )
                xt[chip * DAYS + j] = rows
                return rows

            return lax.fori_loop(first, DAYS, day, rows)

        def chunk_here(k):
            @pl.when(r != k)
            def _():
                arrival(rf.at[k], m_send, m_recv.at[k]).wait_recv()

        chunk_here(0)
        rows = jnp.concatenate(
            [
                atf[pl.ds(pl.multiple_of(c * HALF, HALF), HALF), :] * rf[0, 0:1, :],
                jnp.broadcast_to(rf[0, DAYS : DAYS + 1, :], (8, M)),
            ],
            0,
        )
        xt[0] = rows
        rows = advance(0, 1, rows)
        for k in range(1, CH):
            chunk_here(k)
            rows = advance(k, 0, rows)
        mk[q, c] = rows

        pl.semaphore_wait(barrier, CH - 1 + QN - 1 + RINGS - 1 + 1)

        def ring_send(buf, send, recv, d):
            return copy(buf.at[q, c], buf.at[q, c], send.at[d], recv.at[q], ring_peer(d))

        def ring_share(buf, send, recv, k):
            return copy(buf.at[k, c], buf.at[k, c], send.at[k], recv.at[k], sibling)

        for d in (2, 1, 3):
            ring_send(mk, k_send, k_recv, d).start()
        ring_share(mk, ks_send, ks_recv, q).start()

        def chunk_share(k):
            return copy(xt.at[k * DAYS - 1], pc.at[k - 1], p_send.at[k - 1], p_recv.at[k - 1], sibling)

        for k in range(1, CH):
            chunk_share(k).start()

        weight = 1.0 - scale[...] * jnp.sum(trans[...] * trans[...], axis=0, keepdims=True)

        def back(k, rows):
            return xt[QD - 2 - k] * weight + mm(rows, hphi[0], hplo[0])

        mv[q, c] = lax.fori_loop(0, QD - 1, back, xt[QD - 1] * weight)

        for d in (1, 3, 2):
            k = lax.rem(q + d, QN)
            arrival(mk.at[k, c], k_send.at[d], k_recv.at[k]).wait_recv()
            ring_share(mk, ks_send, ks_recv, k).start()
        for d in (2, 1, 3):
            ring_send(mv, w_send, w_recv, d).start()
        ring_share(mv, ws_send, ws_recv, q).start()
        for k in range(QN):
            ring_share(mk, ks_send, ks_recv, k).wait_recv()
            for half in range(2):
                part = slice(half * HALF, (half + 1) * HALF)
                khi[k, part, :], klo[k, part, :] = split(mk[k, half, 0:HALF, :])
        rows = mk[0, c]
        for k in range(1, QN):
            rows = plus_offset(mm(rows, khi[k], klo[k]), mk[k, 0, HALF : HALF + 1, :])
        nb[x, c] = rows

        def to_peer(d):
            return copy(
                nb.at[x, c], nb.at[x, c], n_send.at[d], n_recv.at[x],
                at(lax.rem(x + d, XN), y, z, c),
            )

        def share(xs):
            return copy(nb.at[xs, c], nb.at[xs, c], ns_send.at[xs], ns_recv.at[xs], sibling)

        for d in (2, 1, 3):
            to_peer(d).start()
        share(x).start()

        def square(k, _):
            h = hp[...]
            h = jnp.dot(h, h, precision=lax.Precision.HIGHEST, preferred_element_type=F32)
            hp[...] = h
            hphi[k], hplo[k] = split(h)
            return 0

        lax.fori_loop(1, POWERS, square, 0)
        ret4[...] = jnp.zeros_like(ret4)
        frc4[...] = jnp.zeros_like(frc4)
        for k in range(CH):
            ret4[:, k, :] = rf[k, 0:DAYS, :]
            frc4[:, k, :] = rf[k, DAYS : 2 * DAYS, :]
        for k in range(1, CH):
            arrival(pc.at[k - 1], p_send.at[k - 1], p_recv.at[k - 1]).wait_recv()
            mine, theirs = split(xt[k * DAYS - 1, 0:HALF, :]), split(pc[k - 1, 0:HALF, :])
            own = pl.ds(pl.multiple_of(c * HALF, HALF), HALF)
            far = pl.ds(pl.multiple_of(other * HALF, HALF), HALF)
            phi[k - 1, own, :], plo[k - 1, own, :] = mine
            phi[k - 1, far, :], plo[k - 1, far, :] = theirs
        for d in (1, 3, 2):
            xs = lax.rem(x + d, XN)
            arrival(nb.at[xs, c], n_send.at[d], n_recv.at[xs]).wait_recv()
            share(xs).start()
        for xs in range(XN):
            share(xs).wait_recv()
            for half in range(2):
                part = slice(half * HALF, (half + 1) * HALF)
                nhi[xs, part, :], nlo[xs, part, :] = split(nb[xs, half, 0:HALF, :])

        def smoother_map():
            for d in (1, 3, 2):
                k = lax.rem(q + d, QN)
                arrival(mv.at[k, c], w_send.at[d], w_recv.at[k]).wait_recv()
                ring_share(mv, ws_send, ws_recv, k).start()
            for k in range(QN):
                ring_share(mv, ws_send, ws_recv, k).wait_recv()
            sm[...] = whole(mv[QN - 1])
            for k in (2, 1, 0):

                @pl.when(q == k)
                def _():
                    vhi[1], vlo[1] = split(sm[0:M, :])
                    vo[1] = sm[M : M + 8, :]

                later = mm(sm[...], hphi[5], hplo[5])
                lhi, llo = split(later[:M])
                sm[...] = (
                    plus_offset(mm(whole(mk[k]), lhi, llo), later[M:]) + whole(mv[k])
                )
            vhi[0], vlo[0] = split(sm[0:M, :])
            vo[0] = sm[M : M + 8, :]

        def group_map():
            tm[...] = whole(nb[0])
            for k in range(1, XN):

                @pl.when(x == k)
                def _():
                    pre[...] = tm[...]

                tm[...] = plus_offset(mm(tm[...], nhi[k], nlo[k]), nb[k, 0, HALF : HALF + 1, :])
            thi[0], tlo[0] = split(tm[0:M, :])
            thi[1], tlo[1] = split(pre[0:M, :])

        def to_group():
            return copy(gout, gin, g_send, g_recv, at(x, lax.rem(y + 1, YN), z, c))

        @pl.when(y == 0)
        def _():
            state = jnp.broadcast_to(init[...], (8, M))
            for k in range(XN):
                ent[k] = state
                state = mm(state, nhi[k], nlo[k]) + nb[k, 0, HALF : HALF + 1, :]
            gout[...] = state
            to_group().start()
            st[0] = ent[x]

        @pl.when(y > 0)
        def _():
            group_map()

        @pl.when(y > 1)
        def _():
            smoother_map()

        @pl.when(y > 0)
        def _():
            arrival(gin, g_send, g_recv).wait_recv()
            gout[...] = mm(gin[...], thi[0], tlo[0]) + tm[M : M + 1, :]

            @pl.when(y < YN - 1)
            def _():
                to_group().start()

            st[0] = jnp.where(
                x == 0, gin[...], mm(gin[...], thi[1], tlo[1]) + pre[M : M + 1, :]
            )

        @pl.when(y < 2)
        def _():
            smoother_map()

        v = (mm(st[0], vhi[0], vlo[0]) + vo[0, 0:1, :])[0:1, :]
        boundary = mm(gout[...], athi[...], atlo[...])
        me = y * XN + x
        vb[me] = jnp.concatenate(
            [v[:, :HALF], v[:, HALF:], boundary[0:1, :HALF], boundary[0:5, HALF:]],
            0,
        )

        def to_plane(k):
            return copy(vb.at[me], vb.at[me], v_send.at[k], v_recv.at[me], plane_peer(k))

        plane = (10, 2, 8, 6, 9, 11, 14, 5, 7, 13, 15, 1, 3, 4, 12)
        for k in plane:
            to_plane(k).start()

        for k in range(1, QN):
            st[k] = mm(st[k - 1], khi[k - 1], klo[k - 1]) + mk[k - 1, 0, HALF : HALF + 1, :]
        state = st[q]
        after = mm(st[lax.min(q + 1, QN - 1)], vhi[1], vlo[1]) + vo[1, 0:1, :]
        fs[...] = jnp.zeros_like(fs)
        fs[0:1, :] = state[0:1, :]
        for k in range(1, CH):
            fs[k : k + 1, :] = (
                mm(state, phi[k - 1], plo[k - 1]) + pc[k - 1, HALF : HALF + 1, :]
            )[0:1, :]
        days = fs[...]
        for j in range(DAYS):
            days = mm(days, athi[...], atlo[...]) * ret4[j] + frc4[j]
            for k in range(CH):
                fb[k * DAYS + j : k * DAYS + j + 1, :] = days[k : k + 1, :]

        @pl.when(c == 0)
        def _():
            fh[...] = fb[:, 0:HALF]

        @pl.when(c == 1)
        def _():
            fh[...] = fb[:, HALF:M]

        def out_copy(src, dst, send, recv, k):
            chip = lax.rem(r + k, CH)
            return copy(
                src.at[pl.ds(pl.multiple_of(chip * DAYS, DAYS), DAYS)], dst, send.at[k], recv,
                at(x, y, q * CH + chip, c),
            )

        own_days = pl.ds(pl.multiple_of(r * DAYS, DAYS), DAYS)

        for k in (3, 2, 1):
            out_copy(fh, frecv, of_send, of_recv, k).start()
        both_out[0:DAYS] = fh[own_days, :]

        sb[0:QD, :] = fb[...] * weight
        sb[QD : 2 * QD, :] = jnp.zeros((QD, M), F32)
        for k in range(5):
            sb[0:QD, :] = sb[0:QD, :] + mm(sb[1 << k : (1 << k) + QD, :], hphi[k], hplo[k])

        eb[...] = jnp.zeros_like(eb)
        for k in plane:
            src = lax.rem(y + k // XN, YN) * XN + lax.rem(x + k % XN, XN)
            arrival(vb.at[src], v_send.at[k], v_recv.at[src]).wait_recv()
        for half in range(2):
            part = slice(half * HALF, (half + 1) * HALF)
            for k in range(1, RINGS):
                eb[k - 1 : k, part] = vb[k, half : half + 1, :]
            eb[RINGS - 1 : RINGS, part] = vb[RINGS - 1, 2 + half : 3 + half, :]
        for k in range(4):
            eb[0:16, :] = eb[0:16, :] + mm(eb[1 << k : (1 << k) + 16, :], hphi[7 + k], hplo[7 + k])
        behind = jnp.broadcast_to(eb[pl.ds(me, 1), :], (8, M))
        left = QN - 1 - q
        behind = jnp.where(lax.rem(left, 2) == 1, mm(behind, hphi[5], hplo[5]), behind)
        behind = jnp.where(left >= 2, mm(behind, hphi[6], hplo[6]), behind)
        behind = jnp.where(left > 0, behind + after, behind)

        wb[QD - 8 : QD, :] = jnp.zeros((8, M), F32)
        wb[QD - 1 : QD, :] = mm(behind, hphi[0], hplo[0])[0:1, :]
        for k in range(5):
            n = 1 << k
            m = max(n, 8)
            wb[QD - 2 * n : QD - n, :] = mm(wb[QD - m : QD, :], hphi[k], hplo[k])[m - n : m, :]
        total = sb[0:QD, :] + wb[...]

        @pl.when(c == 0)
        def _():
            sh[...] = total[:, 0:HALF]

        @pl.when(c == 1)
        def _():
            sh[...] = total[:, HALF:M]

        for k in (3, 2, 1):
            out_copy(sh, srecv, os_send, os_recv, k).start()
        both_out[DAYS:] = sh[own_days, :]

        for d in range(1, QN):
            ring_send(mk, k_send, k_recv, d).wait_send()
            ring_send(mv, w_send, w_recv, d).wait_send()
            chunk_share(d).wait_send()
        for k in range(QN):
            ring_share(mk, ks_send, ks_recv, k).wait_send()
            ring_share(mv, ws_send, ws_recv, k).wait_send()
        for d in range(1, XN):
            to_peer(d).wait_send()
        for xs in range(XN):
            share(xs).wait_send()

        @pl.when(y < YN - 1)
        def _():
            to_group().wait_send()

        for k in plane:
            to_plane(k).wait_send()
        for k in (3, 2, 1):
            out_copy(fh, frecv, of_send, of_recv, k).wait_send()
            out_copy(sh, srecv, os_send, os_recv, k).wait_send()


def shards(observations, masks, gains, transition, smoother_scale, initial_mean):
    hbm, vmem = pl.BlockSpec(memory_space=pltpu.HBM), pl.BlockSpec(memory_space=pltpu.VMEM)
    dma = pltpu.SemaphoreType.DMA

    def buf(*shape, dtype=F32):
        return pltpu.VMEM(shape, dtype)

    def halves(*shape):
        return [buf(*shape, dtype=BF16), buf(*shape, dtype=BF16)]

    out = jax.ShapeDtypeStruct((2 * DAYS, HALF), F32)
    both = pl.pallas_call(
        kernel,
        out_shape=out,
        in_specs=[hbm] * 6,
        out_specs=vmem,
        scratch_shapes=[
            buf(DAYS, M), buf(DAYS, M, dtype=jnp.int32), buf(1, M), buf(M, M), buf(1, M), buf(1, M),
            buf(CH, 2 * DAYS, M), buf(M, M), *halves(M, M),
            buf(M, M), *halves(POWERS, M, M),
            buf(QD, ROWS, M),
            buf(QN, 2, ROWS, M), *halves(QN, M, M),
            buf(QN, 2, ROWS, M), buf(2, 8, M), *halves(2, M, M),
            buf(M + 8, M), buf(M + 8, M), buf(M + 8, M), *halves(2, M, M),
            buf(CH - 1, ROWS, M), *halves(CH - 1, M, M),
            buf(XN, 2, ROWS, M), *halves(XN, M, M),
            buf(DAYS, 8, M), buf(DAYS, 8, M),
            buf(8, M), buf(8, M), buf(XN, 8, M), buf(QN, 8, M),
            buf(8, M), buf(QD, M), buf(2 * QD, M), buf(QD, M),
            buf(RINGS, 8, HALF), buf(32, M),
            buf(QD, HALF), buf(QD, HALF), buf(DAYS, HALF), buf(DAYS, HALF),
            dma((6,)), dma, dma((CH,)),
            dma((QN,)), dma((QN,)), dma((QN,)), dma((QN,)),
            dma((QN,)), dma((QN,)), dma((QN,)), dma((QN,)),
            dma((CH,)), dma((CH,)),
            dma((XN,)), dma((XN,)), dma((XN,)), dma((XN,)),
            dma, dma, dma((RINGS,)), dma((RINGS,)),
            dma((CH,)), dma((CH,)), dma, dma,
        ],
        compiler_params=pltpu.CompilerParams(
            collective_id=0, has_side_effects=True, vmem_limit_bytes=48 * 2**20
        ),
        name="smoother",
    )(
        observations, masks, gains.reshape(1, M), transition,
        smoother_scale.reshape(1, M), initial_mean.reshape(1, M),
    )
    return both[:DAYS], both[DAYS:]


def solution(mesh):
    return jax.shard_map(
        shards,
        mesh=mesh,
        in_specs=(P(("grp", "seg"), None), P(("grp", "seg"), None), P(), P(), P(), P()),
        out_specs=(P(("grp", "seg"), "pair"), P(("grp", "seg"), "pair")),
        check_vma=False,
    )
```

```python
import jax
import jax.numpy as jnp
from jax import lax
from jax.experimental import pallas as pl
from jax.experimental.pallas import tpu as pltpu
from jax.sharding import PartitionSpec as P

F32 = jnp.float32
BF16 = jnp.bfloat16
M = 256
HALF = 128
DAYS = 8
XN, YN, ZN = 4, 4, 16
QN = 4
WORKER = (1, 4, 8, 12)
CH = 4
QD = CH * DAYS
RINGS = XN * YN
POWERS = 11
ROWS = HALF + 8


def split(v):
    hi = v.astype(BF16)
    return hi, (v - hi.astype(F32)).astype(BF16)


def mm(v, whi, wlo):
    rows = v.shape[0]
    if rows % 16 == 8 and rows > 8:
        return jnp.concatenate([mm(v[: rows - 8], whi, wlo), mm(v[rows - 8 :], whi, wlo)], 0)
    hi, lo = split(v)
    both = jnp.dot(jnp.concatenate([hi, lo], 0), whi, preferred_element_type=F32)
    return both[:rows] + both[rows:] + jnp.dot(hi, wlo, preferred_element_type=F32)


def plus_offset(rows, offset):
    n = rows.shape[0] - rows.shape[0] % HALF
    return jnp.concatenate([rows[:n], rows[n:] + offset], 0)


def whole(halves):
    return jnp.concatenate([halves[0, 0:HALF, :], halves[1, 0:HALF, :], halves[0, HALF:ROWS, :]], 0)


def kernel(
    obs_hbm, mask_hbm, gain_hbm, trans_hbm, scale_hbm, init_hbm, both_out,
    obs, mask, gain, trans, scale, init,
    rf, atf, athi, atlo, hp, hphi, hplo, xt, mk, khi, klo, mv, vo, vhi, vlo, sm, tm, pre, thi, tlo, pc, phi, plo,
    exhi, exlo, eyhi, eylo, nb, nhi, nlo, ret4, frc4, gin, gout, ent, st, fs, fb, sb, wb, vb, eb,
    fh, sh, frecv, srecv,
    in_sem, m_send, m_recv, k_send, k_recv, ks_send, ks_recv, w_send, w_recv, ws_send, ws_recv,
    p_send, p_recv, n_send, n_recv, ns_send, ns_recv, g_send, g_recv, v_send, v_recv,
    of_send, os_send, of_recv, os_recv,
):
    seg, y, c = lax.axis_index("seg"), lax.axis_index("grp"), lax.axis_index("pair")
    x, z = lax.div(seg, ZN), lax.rem(seg, ZN)
    q, r = lax.div(z, CH), lax.rem(z, CH)
    other = 1 - c

    def place(k):
        return jnp.where(
            k < 2,
            jnp.where(k == 0, WORKER[0], WORKER[1]),
            jnp.where(k == 2, WORKER[2], WORKER[3]),
        )

    wz = place(q)
    is_worker = z == wz

    fetches = [
        pltpu.make_async_copy(src, dst, in_sem.at[k])
        for k, (src, dst) in enumerate(
            (
                (mask_hbm, mask), (obs_hbm, obs), (gain_hbm, gain),
                (trans_hbm, trans), (scale_hbm, scale), (init_hbm, init),
            )
        )
    ]
    for fetch in fetches:
        fetch.start()

    def at(xx, yy, zz, cc):
        return {"seg": xx * ZN + zz, "grp": yy, "pair": cc}

    sibling = at(x, y, z, other)

    def copy(src, dst, send, recv, where):
        return pltpu.make_async_remote_copy(
            src_ref=src, dst_ref=dst, send_sem=send, recv_sem=recv,
            device_id=where, device_id_type=pl.DeviceIdType.MESH,
        )

    def arrival(dst, send, recv):
        return copy(dst, dst, send, recv, sibling)

    barrier = pltpu.get_barrier_semaphore()

    def greet(where):
        pl.semaphore_signal(
            barrier, inc=1, device_id=where, device_id_type=pl.DeviceIdType.MESH
        )

    def ring_peer(d):
        return at(x, y, place(lax.rem(q + d, QN)), c)

    def plane_peer(k):
        return at(lax.rem(x + k % XN, XN), lax.rem(y + k // XN, YN), z, c)

    @pl.when(is_worker)
    def _():
        for k in range(1, CH):
            greet(at(x, y, q * CH + lax.rem(r + k, CH), c))
        for k in range(1, QN):
            greet(ring_peer(k))
        for k in range(1, RINGS):
            greet(plane_peer(k))
        greet(sibling)

    @pl.when(jnp.logical_not(is_worker))
    def _():
        greet(at(x, y, wz, c))

    for fetch in fetches[:3]:
        fetch.wait()
    observed = mask[...].astype(F32) * gain[...]
    rf[r, 0:DAYS, :] = 1.0 - observed
    rf[r, DAYS : 2 * DAYS, :] = observed * obs[...]

    @pl.when(jnp.logical_not(is_worker))
    def _():
        pl.semaphore_wait(barrier, 1)
        to_worker = copy(rf.at[r], rf.at[r], m_send, m_recv.at[r], at(x, y, wz, c))
        to_worker.start()
        for fetch in fetches[3:]:
            fetch.wait()
        to_worker.wait_send()
        arrival(frecv, m_send, of_recv).wait_recv()
        both_out[0:DAYS] = frecv[...]
        arrival(srecv, m_send, os_recv).wait_recv()
        both_out[DAYS:] = srecv[...]

    @pl.when(is_worker)
    def _():
        for fetch in fetches[3:]:
            fetch.wait()

        at_full = trans[...].T
        atf[...] = at_full
        athi[...], atlo[...] = split(at_full)

        def advance(chip, first, rows):
            def day(j, rows):
                rows = plus_offset(
                    mm(rows, athi[...], atlo[...]) * rf[chip, pl.ds(j, 1), :],
                    rf[chip, pl.ds(DAYS + j, 1), :],
                )
                xt[chip * DAYS + j] = rows
                return rows

            for j in range(first, DAYS):
                rows = day(j, rows)
            return rows

        def chunk_here(k):
            @pl.when(r != k)
            def _():
                arrival(rf.at[k], m_send, m_recv.at[k]).wait_recv()

        chunk_here(0)
        rows = jnp.concatenate(
            [
                atf[pl.ds(pl.multiple_of(c * HALF, HALF), HALF), :] * rf[0, 0:1, :],
                jnp.broadcast_to(rf[0, DAYS : DAYS + 1, :], (8, M)),
            ],
            0,
        )
        xt[0] = rows
        rows = advance(0, 1, rows)
        for k in range(1, CH):
            chunk_here(k)
            rows = advance(k, 0, rows)
        mk[q, c] = rows

        pl.semaphore_wait(barrier, CH - 1 + QN - 1 + RINGS - 1 + 1)

        def ring_send(buf, send, recv, d):
            return copy(buf.at[q, c], buf.at[q, c], send.at[d], recv.at[q], ring_peer(d))

        def ring_share(buf, send, recv, k):
            return copy(buf.at[k, c], buf.at[k, c], send.at[k], recv.at[k], sibling)

        for d in (2, 1, 3):
            ring_send(mk, k_send, k_recv, d).start()
        ring_share(mk, ks_send, ks_recv, q).start()

        def chunk_share(k):
            return copy(xt.at[k * DAYS - 1], pc.at[k - 1], p_send.at[k - 1], p_recv.at[k - 1], sibling)

        h0 = trans[...] * scale[...]
        hp[...] = h0
        hphi[0], hplo[0] = split(h0)

        for k in range(1, CH):
            chunk_share(k).start()

        weight = 1.0 - scale[...] * jnp.sum(trans[...] * trans[...], axis=0, keepdims=True)

        def back(k, rows):
            return xt[QD - 2 - k] * weight + mm(rows, hphi[0], hplo[0])

        mv[q, c] = lax.fori_loop(0, QD - 1, back, xt[QD - 1] * weight)

        for d in (1, 3, 2):
            k = lax.rem(q + d, QN)
            arrival(mk.at[k, c], k_send.at[d], k_recv.at[k]).wait_recv()
            ring_share(mk, ks_send, ks_recv, k).start()
        for d in (2, 1, 3):
            ring_send(mv, w_send, w_recv, d).start()
        ring_share(mv, ws_send, ws_recv, q).start()
        for k in range(QN):
            ring_share(mk, ks_send, ks_recv, k).wait_recv()
            for half in range(2):
                part = slice(half * HALF, (half + 1) * HALF)
                khi[k, part, :], klo[k, part, :] = split(mk[k, half, 0:HALF, :])
        rows = mk[0, c]
        for k in range(1, QN):
            rows = plus_offset(mm(rows, khi[k], klo[k]), mk[k, 0, HALF : HALF + 1, :])
        nb[x, c] = rows

        def to_peer(d):
            return copy(
                nb.at[x, c], nb.at[x, c], n_send.at[d], n_recv.at[x],
                at(lax.rem(x + d, XN), y, z, c),
            )

        def share(xs):
            return copy(nb.at[xs, c], nb.at[xs, c], ns_send.at[xs], ns_recv.at[xs], sibling)

        for d in (2, 1, 3):
            to_peer(d).start()
        share(x).start()

        def square(k, _):
            h = hp[...]
            h = jnp.dot(h, h, precision=lax.Precision.HIGHEST, preferred_element_type=F32)
            hp[...] = h
            hphi[k], hplo[k] = split(h)
            return 0

        lax.fori_loop(1, POWERS, square, 0)

        def power(k):
            return hphi[k].astype(F32) + hplo[k].astype(F32)

        exhi[0], exlo[0] = hphi[0], hplo[0]
        exhi[1], exlo[1] = split(mm(power(3), hphi[0], hplo[0]))
        exhi[2], exlo[2] = split(mm(power(4), hphi[0], hplo[0]))
        exhi[3], exlo[3] = split(mm(power(4), exhi[1], exlo[1]))
        ret4[...] = jnp.zeros_like(ret4)
        frc4[...] = jnp.zeros_like(frc4)
        for k in range(CH):
            ret4[:, k, :] = rf[k, 0:DAYS, :]
            frc4[:, k, :] = rf[k, DAYS : 2 * DAYS, :]
        for k in range(1, CH):
            arrival(pc.at[k - 1], p_send.at[k - 1], p_recv.at[k - 1]).wait_recv()
            mine, theirs = split(xt[k * DAYS - 1, 0:HALF, :]), split(pc[k - 1, 0:HALF, :])
            own = pl.ds(pl.multiple_of(c * HALF, HALF), HALF)
            far = pl.ds(pl.multiple_of(other * HALF, HALF), HALF)
            phi[k - 1, own, :], plo[k - 1, own, :] = mine
            phi[k - 1, far, :], plo[k - 1, far, :] = theirs
        for d in (1, 3, 2):
            xs = lax.rem(x + d, XN)
            arrival(nb.at[xs, c], n_send.at[d], n_recv.at[xs]).wait_recv()
            share(xs).start()
        for xs in range(XN):
            share(xs).wait_recv()
            for half in range(2):
                part = slice(half * HALF, (half + 1) * HALF)
                nhi[xs, part, :], nlo[xs, part, :] = split(nb[xs, half, 0:HALF, :])

        def smoother_map():
            for d in (1, 3, 2):
                k = lax.rem(q + d, QN)
                arrival(mv.at[k, c], w_send.at[d], w_recv.at[k]).wait_recv()
                ring_share(mv, ws_send, ws_recv, k).start()
            for k in range(QN):
                ring_share(mv, ws_send, ws_recv, k).wait_recv()
            sm[...] = whole(mv[QN - 1])
            for k in (2, 1, 0):

                @pl.when(q == k)
                def _():
                    vhi[1], vlo[1] = split(sm[0:M, :])
                    vo[1] = sm[M : M + 8, :]

                later = mm(sm[...], hphi[5], hplo[5])
                lhi, llo = split(later[:M])
                sm[...] = (
                    plus_offset(mm(whole(mk[k]), lhi, llo), later[M:]) + whole(mv[k])
                )
            vhi[0], vlo[0] = split(sm[0:M, :])
            vo[0] = sm[M : M + 8, :]

        def group_map():
            tm[...] = whole(nb[0])
            for k in range(1, XN):

                @pl.when(x == k)
                def _():
                    pre[...] = tm[...]

                tm[...] = plus_offset(mm(tm[...], nhi[k], nlo[k]), nb[k, 0, HALF : HALF + 1, :])
            thi[0], tlo[0] = split(tm[0:M, :])
            thi[1], tlo[1] = split(pre[0:M, :])

        def to_group():
            return copy(gout, gin, g_send, g_recv, at(x, lax.rem(y + 1, YN), z, c))

        left = QN - 1 - q

        def behind_quads():
            def fold(k, _):
                for bit in range(2):
                    src = (exhi, exlo) if bit == 0 else (eyhi, eylo)

                    @pl.when(lax.rem(lax.div(left, 1 << bit), 2) == 1)
                    def _():
                        whole_map = src[0][k].astype(F32) + src[1][k].astype(F32)
                        eyhi[k], eylo[k] = split(mm(whole_map, hphi[5 + bit], hplo[5 + bit]))

                    if bit == 0:

                        @pl.when(lax.rem(left, 2) == 0)
                        def _():
                            eyhi[k], eylo[k] = exhi[k], exlo[k]

                return 0

            lax.fori_loop(0, CH, fold, 0)

        def expand(vector, xhi, xlo):
            first = jnp.concatenate(
                [mm(vector, xhi[k], xlo[k])[0:1, :] for k in range(CH)]
                + [jnp.zeros((8 - CH, M), F32)],
                0,
            )
            found = first
            for k in range(3):
                found = jnp.concatenate([found, mm(found, hphi[k], hplo[k])], 0)
            for k in range(CH):
                for j in range(DAYS):
                    t = QD - 1 - DAYS * k - j
                    wb[t : t + 1, :] = found[8 * j + k : 8 * j + k + 1, :]

        @pl.when(y == 0)
        def _():
            state = jnp.broadcast_to(init[...], (8, M))
            for k in range(XN):
                ent[k] = state
                state = mm(state, nhi[k], nlo[k]) + nb[k, 0, HALF : HALF + 1, :]
            gout[...] = state
            to_group().start()
            st[0] = ent[x]

        @pl.when(y > 0)
        def _():
            group_map()

        @pl.when(y > 1)
        def _():
            smoother_map()

        @pl.when(y == YN - 1)
        def _():
            behind_quads()

        @pl.when(y > 0)
        def _():
            arrival(gin, g_send, g_recv).wait_recv()
            gout[...] = mm(gin[...], thi[0], tlo[0]) + tm[M : M + 1, :]

            @pl.when(y < YN - 1)
            def _():
                to_group().start()

            st[0] = jnp.where(
                x == 0, gin[...], mm(gin[...], thi[1], tlo[1]) + pre[M : M + 1, :]
            )

        @pl.when(y < 2)
        def _():
            smoother_map()

        v = (mm(st[0], vhi[0], vlo[0]) + vo[0, 0:1, :])[0:1, :]
        boundary = mm(gout[...], athi[...], atlo[...])
        me = y * XN + x
        vb[me] = jnp.concatenate(
            [v[:, :HALF], v[:, HALF:], boundary[0:1, :HALF], boundary[0:5, HALF:]],
            0,
        )

        def to_plane(k):
            return copy(vb.at[me], vb.at[me], v_send.at[k], v_recv.at[me], plane_peer(k))

        plane = (10, 2, 8, 6, 9, 11, 14, 5, 7, 13, 15, 1, 3, 4, 12)
        for k in plane:
            to_plane(k).start()

        for k in range(1, QN):
            st[k] = mm(st[k - 1], khi[k - 1], klo[k - 1]) + mk[k - 1, 0, HALF : HALF + 1, :]
        state = st[q]
        after = mm(st[lax.min(q + 1, QN - 1)], vhi[1], vlo[1]) + vo[1, 0:1, :]
        fs[...] = jnp.zeros_like(fs)
        fs[0:1, :] = state[0:1, :]
        for k in range(1, CH):
            fs[k : k + 1, :] = (
                mm(state, phi[k - 1], plo[k - 1]) + pc[k - 1, HALF : HALF + 1, :]
            )[0:1, :]
        days = fs[...]
        for j in range(DAYS):
            days = mm(days, athi[...], atlo[...]) * ret4[j] + frc4[j]
            for k in range(CH):
                fb[k * DAYS + j : k * DAYS + j + 1, :] = days[k : k + 1, :]

        @pl.when(c == 0)
        def _():
            fh[...] = fb[:, 0:HALF]

        @pl.when(c == 1)
        def _():
            fh[...] = fb[:, HALF:M]

        def out_copy(src, dst, send, recv, k):
            chip = lax.rem(r + k, CH)
            return copy(
                src.at[pl.ds(pl.multiple_of(chip * DAYS, DAYS), DAYS)], dst, send.at[k], recv,
                at(x, y, q * CH + chip, c),
            )

        own_days = pl.ds(pl.multiple_of(r * DAYS, DAYS), DAYS)

        for k in (3, 2, 1):
            out_copy(fh, frecv, of_send, of_recv, k).start()
        both_out[0:DAYS] = fh[own_days, :]

        sb[0:QD, :] = fb[...] * weight
        sb[QD : 2 * QD, :] = jnp.zeros((QD, M), F32)
        for k in range(5):
            sb[0:QD, :] = sb[0:QD, :] + mm(sb[1 << k : (1 << k) + QD, :], hphi[k], hplo[k])

        @pl.when(y < YN - 1)
        def _():
            behind_quads()

        expand(jnp.where(left > 0, after, 0.0), exhi, exlo)
        sb[0:QD, :] = sb[0:QD, :] + wb[...]

        eb[...] = jnp.zeros_like(eb)
        for k in plane:
            src = lax.rem(y + k // XN, YN) * XN + lax.rem(x + k % XN, XN)
            arrival(vb.at[src], v_send.at[k], v_recv.at[src]).wait_recv()
        for half in range(2):
            part = slice(half * HALF, (half + 1) * HALF)
            for k in range(1, RINGS):
                eb[k - 1 : k, part] = vb[k, half : half + 1, :]
            eb[RINGS - 1 : RINGS, part] = vb[RINGS - 1, 2 + half : 3 + half, :]
        for k in range(4):
            eb[0:16, :] = eb[0:16, :] + mm(eb[1 << k : (1 << k) + 16, :], hphi[7 + k], hplo[7 + k])
        behind = jnp.broadcast_to(eb[pl.ds(me, 1), :], (8, M))
        expand(behind, eyhi, eylo)
        total = sb[0:QD, :] + wb[...]

        @pl.when(c == 0)
        def _():
            sh[...] = total[:, 0:HALF]

        @pl.when(c == 1)
        def _():
            sh[...] = total[:, HALF:M]

        for k in (3, 2, 1):
            out_copy(sh, srecv, os_send, os_recv, k).start()
        both_out[DAYS:] = sh[own_days, :]

        for d in range(1, QN):
            ring_send(mk, k_send, k_recv, d).wait_send()
            ring_send(mv, w_send, w_recv, d).wait_send()
            chunk_share(d).wait_send()
        for k in range(QN):
            ring_share(mk, ks_send, ks_recv, k).wait_send()
            ring_share(mv, ws_send, ws_recv, k).wait_send()
        for d in range(1, XN):
            to_peer(d).wait_send()
        for xs in range(XN):
            share(xs).wait_send()

        @pl.when(y < YN - 1)
        def _():
            to_group().wait_send()

        for k in plane:
            to_plane(k).wait_send()
        for k in (3, 2, 1):
            out_copy(fh, frecv, of_send, of_recv, k).wait_send()
            out_copy(sh, srecv, os_send, os_recv, k).wait_send()


def shards(observations, masks, gains, transition, smoother_scale, initial_mean):
    hbm, vmem = pl.BlockSpec(memory_space=pltpu.HBM), pl.BlockSpec(memory_space=pltpu.VMEM)
    dma = pltpu.SemaphoreType.DMA

    def buf(*shape, dtype=F32):
        return pltpu.VMEM(shape, dtype)

    def halves(*shape):
        return [buf(*shape, dtype=BF16), buf(*shape, dtype=BF16)]

    out = jax.ShapeDtypeStruct((2 * DAYS, HALF), F32)
    both = pl.pallas_call(
        kernel,
        out_shape=out,
        in_specs=[hbm] * 6,
        out_specs=vmem,
        scratch_shapes=[
            buf(DAYS, M), buf(DAYS, M, dtype=jnp.int32), buf(1, M), buf(M, M), buf(1, M), buf(1, M),
            buf(CH, 2 * DAYS, M), buf(M, M), *halves(M, M),
            buf(M, M), *halves(POWERS, M, M),
            buf(QD, ROWS, M),
            buf(QN, 2, ROWS, M), *halves(QN, M, M),
            buf(QN, 2, ROWS, M), buf(2, 8, M), *halves(2, M, M),
            buf(M + 8, M), buf(M + 8, M), buf(M + 8, M), *halves(2, M, M),
            buf(CH - 1, ROWS, M), *halves(CH - 1, M, M),
            *halves(CH, M, M), *halves(CH, M, M),
            buf(XN, 2, ROWS, M), *halves(XN, M, M),
            buf(DAYS, 8, M), buf(DAYS, 8, M),
            buf(8, M), buf(8, M), buf(XN, 8, M), buf(QN, 8, M),
            buf(8, M), buf(QD, M), buf(2 * QD, M), buf(QD, M),
            buf(RINGS, 8, HALF), buf(32, M),
            buf(QD, HALF), buf(QD, HALF), buf(DAYS, HALF), buf(DAYS, HALF),
            dma((6,)), dma, dma((CH,)),
            dma((QN,)), dma((QN,)), dma((QN,)), dma((QN,)),
            dma((QN,)), dma((QN,)), dma((QN,)), dma((QN,)),
            dma((CH,)), dma((CH,)),
            dma((XN,)), dma((XN,)), dma((XN,)), dma((XN,)),
            dma, dma, dma((RINGS,)), dma((RINGS,)),
            dma((CH,)), dma((CH,)), dma, dma,
        ],
        compiler_params=pltpu.CompilerParams(
            collective_id=0, has_side_effects=True, vmem_limit_bytes=48 * 2**20
        ),
        name="smoother",
    )(
        observations, masks, gains.reshape(1, M), transition,
        smoother_scale.reshape(1, M), initial_mean.reshape(1, M),
    )
    return both[:DAYS], both[DAYS:]


def solution(mesh):
    return jax.shard_map(
        shards,
        mesh=mesh,
        in_specs=(P(("grp", "seg"), None), P(("grp", "seg"), None), P(), P(), P(), P()),
        out_specs=(P(("grp", "seg"), "pair"), P(("grp", "seg"), "pair")),
        check_vma=False,
    )
```

```python
import jax
import jax.numpy as jnp
from jax import lax
from jax.experimental import pallas as pl
from jax.experimental.pallas import tpu as pltpu
from jax.sharding import PartitionSpec as P

F32 = jnp.float32
BF16 = jnp.bfloat16
M = 256
HALF = 128
DAYS = 8
XN, YN, ZN = 4, 4, 16
QN = 4
WORKER = (1, 4, 8, 12)
CH = 4
QD = CH * DAYS
RINGS = XN * YN
POWERS = 11
ROWS = HALF + 8


def split(v):
    hi = v.astype(BF16)
    return hi, (v - hi.astype(F32)).astype(BF16)


def mm(v, whi, wlo):
    rows = v.shape[0]
    if rows == ROWS:
        cuts = (0, HALF // 2, HALF, ROWS)
        return jnp.concatenate([mm(v[i:j], whi, wlo) for i, j in zip(cuts, cuts[1:])], 0)
    if rows % 16 == 8 and rows > 8:
        return jnp.concatenate([mm(v[: rows - 8], whi, wlo), mm(v[rows - 8 :], whi, wlo)], 0)
    hi, lo = split(v)
    both = jnp.dot(jnp.concatenate([hi, lo], 0), whi, preferred_element_type=F32)
    return both[:rows] + both[rows:] + jnp.dot(hi, wlo, preferred_element_type=F32)


def plus_offset(rows, offset):
    n = rows.shape[0] - rows.shape[0] % HALF
    return jnp.concatenate([rows[:n], rows[n:] + offset], 0)


def whole(halves):
    return jnp.concatenate([halves[0, 0:HALF, :], halves[1, 0:HALF, :], halves[0, HALF:ROWS, :]], 0)


def kernel(
    obs_hbm, mask_hbm, gain_hbm, trans_hbm, scale_hbm, init_hbm, both_out,
    obs, mask, gain, trans, scale, init,
    rf, atf, athi, atlo, hp, hphi, hplo, xt, mk, khi, klo, mv, vo, vhi, vlo, sm, tm, pre, thi, tlo, pc, phi, plo,
    exhi, exlo, eyhi, eylo, nb, nhi, nlo, ret4, frc4, gin, gout, ent, st, fs, fb, sb, wb, vb, eb,
    fh, sh, frecv, srecv,
    in_sem, m_send, m_recv, k_send, k_recv, ks_send, ks_recv, w_send, w_recv, ws_send, ws_recv,
    p_send, p_recv, n_send, n_recv, ns_send, ns_recv, g_send, g_recv, v_send, v_recv,
    of_send, os_send, of_recv, os_recv,
):
    seg, y, c = lax.axis_index("seg"), lax.axis_index("grp"), lax.axis_index("pair")
    x, z = lax.div(seg, ZN), lax.rem(seg, ZN)
    q, r = lax.div(z, CH), lax.rem(z, CH)
    other = 1 - c

    def place(k):
        return jnp.where(
            k < 2,
            jnp.where(k == 0, WORKER[0], WORKER[1]),
            jnp.where(k == 2, WORKER[2], WORKER[3]),
        )

    wz = place(q)
    is_worker = z == wz

    fetches = [
        pltpu.make_async_copy(src, dst, in_sem.at[k])
        for k, (src, dst) in enumerate(
            (
                (mask_hbm, mask), (obs_hbm, obs), (gain_hbm, gain),
                (trans_hbm, trans), (scale_hbm, scale), (init_hbm, init),
            )
        )
    ]
    for fetch in fetches:
        fetch.start()

    def at(xx, yy, zz, cc):
        return {"seg": xx * ZN + zz, "grp": yy, "pair": cc}

    sibling = at(x, y, z, other)

    def copy(src, dst, send, recv, where):
        return pltpu.make_async_remote_copy(
            src_ref=src, dst_ref=dst, send_sem=send, recv_sem=recv,
            device_id=where, device_id_type=pl.DeviceIdType.MESH,
        )

    def arrival(dst, send, recv):
        return copy(dst, dst, send, recv, sibling)

    barrier = pltpu.get_barrier_semaphore()

    def greet(where):
        pl.semaphore_signal(
            barrier, inc=1, device_id=where, device_id_type=pl.DeviceIdType.MESH
        )

    def ring_peer(d):
        return at(x, y, place(lax.rem(q + d, QN)), c)

    def plane_peer(k):
        return at(lax.rem(x + k % XN, XN), lax.rem(y + k // XN, YN), z, c)

    @pl.when(is_worker)
    def _():
        for k in range(1, CH):
            greet(at(x, y, q * CH + lax.rem(r + k, CH), c))
        for k in range(1, QN):
            greet(ring_peer(k))
        for k in range(1, RINGS):
            greet(plane_peer(k))
        greet(sibling)

    @pl.when(jnp.logical_not(is_worker))
    def _():
        greet(at(x, y, wz, c))

    for fetch in fetches[:3]:
        fetch.wait()
    observed = mask[...].astype(F32) * gain[...]
    rf[r, 0:DAYS, :] = 1.0 - observed
    rf[r, DAYS : 2 * DAYS, :] = observed * obs[...]

    @pl.when(jnp.logical_not(is_worker))
    def _():
        pl.semaphore_wait(barrier, 1)
        to_worker = copy(rf.at[r], rf.at[r], m_send, m_recv.at[r], at(x, y, wz, c))
        to_worker.start()
        for fetch in fetches[3:]:
            fetch.wait()
        to_worker.wait_send()
        arrival(frecv, m_send, of_recv).wait_recv()
        both_out[0:DAYS] = frecv[...]
        arrival(srecv, m_send, os_recv).wait_recv()
        both_out[DAYS:] = srecv[...]

    @pl.when(is_worker)
    def _():
        for fetch in fetches[3:]:
            fetch.wait()

        at_full = trans[...].T
        atf[...] = at_full
        athi[...], atlo[...] = split(at_full)

        def advance(chip, first, rows):
            def day(j, rows):
                rows = plus_offset(
                    mm(rows, athi[...], atlo[...]) * rf[chip, pl.ds(j, 1), :],
                    rf[chip, pl.ds(DAYS + j, 1), :],
                )
                xt[chip * DAYS + j] = rows
                return rows

            for j in range(first, DAYS):
                rows = day(j, rows)
            return rows

        def chunk_here(k):
            @pl.when(r != k)
            def _():
                arrival(rf.at[k], m_send, m_recv.at[k]).wait_recv()

        chunk_here(0)
        rows = jnp.concatenate(
            [
                atf[pl.ds(pl.multiple_of(c * HALF, HALF), HALF), :] * rf[0, 0:1, :],
                jnp.broadcast_to(rf[0, DAYS : DAYS + 1, :], (8, M)),
            ],
            0,
        )
        xt[0] = rows
        rows = advance(0, 1, rows)
        for k in range(1, CH):
            chunk_here(k)
            rows = advance(k, 0, rows)
        mk[q, c] = rows

        pl.semaphore_wait(barrier, CH - 1 + QN - 1 + RINGS - 1 + 1)

        def ring_send(buf, send, recv, d):
            return copy(buf.at[q, c], buf.at[q, c], send.at[d], recv.at[q], ring_peer(d))

        def ring_share(buf, send, recv, k):
            return copy(buf.at[k, c], buf.at[k, c], send.at[k], recv.at[k], sibling)

        for d in (2, 1, 3):
            ring_send(mk, k_send, k_recv, d).start()
        ring_share(mk, ks_send, ks_recv, q).start()

        def chunk_share(k):
            return copy(xt.at[k * DAYS - 1], pc.at[k - 1], p_send.at[k - 1], p_recv.at[k - 1], sibling)

        h0 = trans[...] * scale[...]
        hp[...] = h0
        hphi[0], hplo[0] = split(h0)

        for k in range(1, CH):
            chunk_share(k).start()

        weight = 1.0 - scale[...] * jnp.sum(trans[...] * trans[...], axis=0, keepdims=True)

        def back(k, rows):
            return xt[QD - 2 - k] * weight + mm(rows, hphi[0], hplo[0])

        mv[q, c] = lax.fori_loop(0, QD - 1, back, xt[QD - 1] * weight)

        for d in (1, 3, 2):
            k = lax.rem(q + d, QN)
            arrival(mk.at[k, c], k_send.at[d], k_recv.at[k]).wait_recv()
            ring_share(mk, ks_send, ks_recv, k).start()
        for d in (2, 1, 3):
            ring_send(mv, w_send, w_recv, d).start()
        ring_share(mv, ws_send, ws_recv, q).start()
        for k in range(QN):
            ring_share(mk, ks_send, ks_recv, k).wait_recv()
            for half in range(2):
                part = slice(half * HALF, (half + 1) * HALF)
                khi[k, part, :], klo[k, part, :] = split(mk[k, half, 0:HALF, :])
        rows = mk[0, c]
        for k in range(1, QN):
            rows = plus_offset(mm(rows, khi[k], klo[k]), mk[k, 0, HALF : HALF + 1, :])
        nb[x, c] = rows

        def to_peer(d):
            return copy(
                nb.at[x, c], nb.at[x, c], n_send.at[d], n_recv.at[x],
                at(lax.rem(x + d, XN), y, z, c),
            )

        def share(xs):
            return copy(nb.at[xs, c], nb.at[xs, c], ns_send.at[xs], ns_recv.at[xs], sibling)

        for d in (2, 1, 3):
            to_peer(d).start()
        share(x).start()

        def square(k, _):
            h = hp[...]
            h = jnp.dot(h, h, precision=lax.Precision.HIGHEST, preferred_element_type=F32)
            hp[...] = h
            hphi[k], hplo[k] = split(h)
            return 0

        lax.fori_loop(1, POWERS, square, 0)

        def power(k):
            return hphi[k].astype(F32) + hplo[k].astype(F32)

        exhi[0], exlo[0] = hphi[0], hplo[0]
        exhi[1], exlo[1] = split(mm(power(3), hphi[0], hplo[0]))
        exhi[2], exlo[2] = split(mm(power(4), hphi[0], hplo[0]))
        exhi[3], exlo[3] = split(mm(power(4), exhi[1], exlo[1]))
        ret4[...] = jnp.zeros_like(ret4)
        frc4[...] = jnp.zeros_like(frc4)
        for k in range(CH):
            ret4[:, k, :] = rf[k, 0:DAYS, :]
            frc4[:, k, :] = rf[k, DAYS : 2 * DAYS, :]
        for k in range(1, CH):
            arrival(pc.at[k - 1], p_send.at[k - 1], p_recv.at[k - 1]).wait_recv()
            mine, theirs = split(xt[k * DAYS - 1, 0:HALF, :]), split(pc[k - 1, 0:HALF, :])
            own = pl.ds(pl.multiple_of(c * HALF, HALF), HALF)
            far = pl.ds(pl.multiple_of(other * HALF, HALF), HALF)
            phi[k - 1, own, :], plo[k - 1, own, :] = mine
            phi[k - 1, far, :], plo[k - 1, far, :] = theirs
        for d in (1, 3, 2):
            xs = lax.rem(x + d, XN)
            arrival(nb.at[xs, c], n_send.at[d], n_recv.at[xs]).wait_recv()
            share(xs).start()
        for xs in range(XN):
            share(xs).wait_recv()
            for half in range(2):
                part = slice(half * HALF, (half + 1) * HALF)
                nhi[xs, part, :], nlo[xs, part, :] = split(nb[xs, half, 0:HALF, :])

        def smoother_map():
            for d in (1, 3, 2):
                k = lax.rem(q + d, QN)
                arrival(mv.at[k, c], w_send.at[d], w_recv.at[k]).wait_recv()
                ring_share(mv, ws_send, ws_recv, k).start()
            for k in range(QN):
                ring_share(mv, ws_send, ws_recv, k).wait_recv()
            sm[...] = whole(mv[QN - 1])
            for k in (2, 1, 0):

                @pl.when(q == k)
                def _():
                    vhi[1], vlo[1] = split(sm[0:M, :])
                    vo[1] = sm[M : M + 8, :]

                later = mm(sm[...], hphi[5], hplo[5])
                lhi, llo = split(later[:M])
                sm[...] = (
                    plus_offset(mm(whole(mk[k]), lhi, llo), later[M:]) + whole(mv[k])
                )
            vhi[0], vlo[0] = split(sm[0:M, :])
            vo[0] = sm[M : M + 8, :]

        def group_map():
            tm[...] = whole(nb[0])
            for k in range(1, XN):

                @pl.when(x == k)
                def _():
                    pre[...] = tm[...]

                tm[...] = plus_offset(mm(tm[...], nhi[k], nlo[k]), nb[k, 0, HALF : HALF + 1, :])
            thi[0], tlo[0] = split(tm[0:M, :])
            thi[1], tlo[1] = split(pre[0:M, :])

        def to_group():
            return copy(gout, gin, g_send, g_recv, at(x, lax.rem(y + 1, YN), z, c))

        left = QN - 1 - q

        def behind_quads():
            def fold(k, _):
                for bit in range(2):
                    src = (exhi, exlo) if bit == 0 else (eyhi, eylo)

                    @pl.when(lax.rem(lax.div(left, 1 << bit), 2) == 1)
                    def _():
                        whole_map = src[0][k].astype(F32) + src[1][k].astype(F32)
                        eyhi[k], eylo[k] = split(mm(whole_map, hphi[5 + bit], hplo[5 + bit]))

                    if bit == 0:

                        @pl.when(lax.rem(left, 2) == 0)
                        def _():
                            eyhi[k], eylo[k] = exhi[k], exlo[k]

                return 0

            lax.fori_loop(0, CH, fold, 0)

        def expand(vector, xhi, xlo):
            first = jnp.concatenate(
                [mm(vector, xhi[k], xlo[k])[0:1, :] for k in range(CH)]
                + [jnp.zeros((8 - CH, M), F32)],
                0,
            )
            found = first
            for k in range(3):
                found = jnp.concatenate([found, mm(found, hphi[k], hplo[k])], 0)
            for k in range(CH):
                for j in range(DAYS):
                    t = QD - 1 - DAYS * k - j
                    wb[t : t + 1, :] = found[8 * j + k : 8 * j + k + 1, :]

        @pl.when(y == 0)
        def _():
            state = jnp.broadcast_to(init[...], (8, M))
            for k in range(XN):
                ent[k] = state
                state = mm(state, nhi[k], nlo[k]) + nb[k, 0, HALF : HALF + 1, :]
            gout[...] = state
            to_group().start()
            st[0] = ent[x]

        @pl.when(y > 0)
        def _():
            group_map()

        @pl.when(y > 1)
        def _():
            smoother_map()

        @pl.when(y == YN - 1)
        def _():
            behind_quads()

        @pl.when(y > 0)
        def _():
            arrival(gin, g_send, g_recv).wait_recv()
            gout[...] = mm(gin[...], thi[0], tlo[0]) + tm[M : M + 1, :]

            @pl.when(y < YN - 1)
            def _():
                to_group().start()

            st[0] = jnp.where(
                x == 0, gin[...], mm(gin[...], thi[1], tlo[1]) + pre[M : M + 1, :]
            )

        @pl.when(y < 2)
        def _():
            smoother_map()

        v = (mm(st[0], vhi[0], vlo[0]) + vo[0, 0:1, :])[0:1, :]
        boundary = mm(gout[...], athi[...], atlo[...])
        me = y * XN + x
        vb[me] = jnp.concatenate(
            [v[:, :HALF], v[:, HALF:], boundary[0:1, :HALF], boundary[0:5, HALF:]],
            0,
        )

        def to_plane(k):
            return copy(vb.at[me], vb.at[me], v_send.at[k], v_recv.at[me], plane_peer(k))

        plane = (10, 2, 8, 6, 9, 11, 14, 5, 7, 13, 15, 1, 3, 4, 12)
        for k in plane:
            to_plane(k).start()

        for k in range(1, QN):
            st[k] = mm(st[k - 1], khi[k - 1], klo[k - 1]) + mk[k - 1, 0, HALF : HALF + 1, :]
        state = st[q]
        after = mm(st[lax.min(q + 1, QN - 1)], vhi[1], vlo[1]) + vo[1, 0:1, :]
        fs[...] = jnp.zeros_like(fs)
        fs[0:1, :] = state[0:1, :]
        for k in range(1, CH):
            fs[k : k + 1, :] = (
                mm(state, phi[k - 1], plo[k - 1]) + pc[k - 1, HALF : HALF + 1, :]
            )[0:1, :]
        days = fs[...]
        for j in range(DAYS):
            days = mm(days, athi[...], atlo[...]) * ret4[j] + frc4[j]
            for k in range(CH):
                fb[k * DAYS + j : k * DAYS + j + 1, :] = days[k : k + 1, :]

        @pl.when(c == 0)
        def _():
            fh[...] = fb[:, 0:HALF]

        @pl.when(c == 1)
        def _():
            fh[...] = fb[:, HALF:M]

        def out_copy(src, dst, send, recv, k):
            chip = lax.rem(r + k, CH)
            return copy(
                src.at[pl.ds(pl.multiple_of(chip * DAYS, DAYS), DAYS)], dst, send.at[k], recv,
                at(x, y, q * CH + chip, c),
            )

        own_days = pl.ds(pl.multiple_of(r * DAYS, DAYS), DAYS)

        for k in (3, 2, 1):
            out_copy(fh, frecv, of_send, of_recv, k).start()
        both_out[0:DAYS] = fh[own_days, :]

        sb[0:QD, :] = fb[...] * weight
        sb[QD : 2 * QD, :] = jnp.zeros((QD, M), F32)
        for k in range(5):
            sb[0:QD, :] = sb[0:QD, :] + mm(sb[1 << k : (1 << k) + QD, :], hphi[k], hplo[k])

        @pl.when(y < YN - 1)
        def _():
            behind_quads()

        expand(jnp.where(left > 0, after, 0.0), exhi, exlo)
        sb[0:QD, :] = sb[0:QD, :] + wb[...]

        eb[...] = jnp.zeros_like(eb)
        for k in plane:
            src = lax.rem(y + k // XN, YN) * XN + lax.rem(x + k % XN, XN)
            arrival(vb.at[src], v_send.at[k], v_recv.at[src]).wait_recv()
        for half in range(2):
            part = slice(half * HALF, (half + 1) * HALF)
            for k in range(1, RINGS):
                eb[k - 1 : k, part] = vb[k, half : half + 1, :]
            eb[RINGS - 1 : RINGS, part] = vb[RINGS - 1, 2 + half : 3 + half, :]
        for k in range(4):
            eb[0:16, :] = eb[0:16, :] + mm(eb[1 << k : (1 << k) + 16, :], hphi[7 + k], hplo[7 + k])
        behind = jnp.broadcast_to(eb[pl.ds(me, 1), :], (8, M))
        expand(behind, eyhi, eylo)
        total = sb[0:QD, :] + wb[...]

        @pl.when(c == 0)
        def _():
            sh[...] = total[:, 0:HALF]

        @pl.when(c == 1)
        def _():
            sh[...] = total[:, HALF:M]

        for k in (3, 2, 1):
            out_copy(sh, srecv, os_send, os_recv, k).start()
        both_out[DAYS:] = sh[own_days, :]

        for d in range(1, QN):
            ring_send(mk, k_send, k_recv, d).wait_send()
            ring_send(mv, w_send, w_recv, d).wait_send()
            chunk_share(d).wait_send()
        for k in range(QN):
            ring_share(mk, ks_send, ks_recv, k).wait_send()
            ring_share(mv, ws_send, ws_recv, k).wait_send()
        for d in range(1, XN):
            to_peer(d).wait_send()
        for xs in range(XN):
            share(xs).wait_send()

        @pl.when(y < YN - 1)
        def _():
            to_group().wait_send()

        for k in plane:
            to_plane(k).wait_send()
        for k in (3, 2, 1):
            out_copy(fh, frecv, of_send, of_recv, k).wait_send()
            out_copy(sh, srecv, os_send, os_recv, k).wait_send()


def shards(observations, masks, gains, transition, smoother_scale, initial_mean):
    hbm, vmem = pl.BlockSpec(memory_space=pltpu.HBM), pl.BlockSpec(memory_space=pltpu.VMEM)
    dma = pltpu.SemaphoreType.DMA

    def buf(*shape, dtype=F32):
        return pltpu.VMEM(shape, dtype)

    def halves(*shape):
        return [buf(*shape, dtype=BF16), buf(*shape, dtype=BF16)]

    out = jax.ShapeDtypeStruct((2 * DAYS, HALF), F32)
    both = pl.pallas_call(
        kernel,
        out_shape=out,
        in_specs=[hbm] * 6,
        out_specs=vmem,
        scratch_shapes=[
            buf(DAYS, M), buf(DAYS, M, dtype=jnp.int32), buf(1, M), buf(M, M), buf(1, M), buf(1, M),
            buf(CH, 2 * DAYS, M), buf(M, M), *halves(M, M),
            buf(M, M), *halves(POWERS, M, M),
            buf(QD, ROWS, M),
            buf(QN, 2, ROWS, M), *halves(QN, M, M),
            buf(QN, 2, ROWS, M), buf(2, 8, M), *halves(2, M, M),
            buf(M + 8, M), buf(M + 8, M), buf(M + 8, M), *halves(2, M, M),
            buf(CH - 1, ROWS, M), *halves(CH - 1, M, M),
            *halves(CH, M, M), *halves(CH, M, M),
            buf(XN, 2, ROWS, M), *halves(XN, M, M),
            buf(DAYS, 8, M), buf(DAYS, 8, M),
            buf(8, M), buf(8, M), buf(XN, 8, M), buf(QN, 8, M),
            buf(8, M), buf(QD, M), buf(2 * QD, M), buf(QD, M),
            buf(RINGS, 8, HALF), buf(32, M),
            buf(QD, HALF), buf(QD, HALF), buf(DAYS, HALF), buf(DAYS, HALF),
            dma((6,)), dma, dma((CH,)),
            dma((QN,)), dma((QN,)), dma((QN,)), dma((QN,)),
            dma((QN,)), dma((QN,)), dma((QN,)), dma((QN,)),
            dma((CH,)), dma((CH,)),
            dma((XN,)), dma((XN,)), dma((XN,)), dma((XN,)),
            dma, dma, dma((RINGS,)), dma((RINGS,)),
            dma((CH,)), dma((CH,)), dma, dma,
        ],
        compiler_params=pltpu.CompilerParams(
            collective_id=0, has_side_effects=True, vmem_limit_bytes=48 * 2**20
        ),
        name="smoother",
    )(
        observations, masks, gains.reshape(1, M), transition,
        smoother_scale.reshape(1, M), initial_mean.reshape(1, M),
    )
    return both[:DAYS], both[DAYS:]


def solution(mesh):
    return jax.shard_map(
        shards,
        mesh=mesh,
        in_specs=(P(("grp", "seg"), None), P(("grp", "seg"), None), P(), P(), P(), P()),
        out_specs=(P(("grp", "seg"), "pair"), P(("grp", "seg"), "pair")),
        check_vma=False,
    )
```

```python
import jax
import jax.numpy as jnp
from jax import lax
from jax.experimental import pallas as pl
from jax.experimental.pallas import tpu as pltpu
from jax.sharding import PartitionSpec as P

F32 = jnp.float32
BF16 = jnp.bfloat16
M = 256
HALF = 128
DAYS = 8
XN, YN, ZN = 4, 4, 16
QN = 4
WORKER = (1, 4, 8, 12)
CH = 4
QD = CH * DAYS
RINGS = XN * YN
POWERS = 11
ROWS = HALF + 8


def split(v):
    hi = v.astype(BF16)
    return hi, (v - hi.astype(F32)).astype(BF16)


def mm(v, whi, wlo):
    rows = v.shape[0]
    if rows == ROWS:
        cuts = (0, HALF // 2, HALF, ROWS)
        return jnp.concatenate([mm(v[i:j], whi, wlo) for i, j in zip(cuts, cuts[1:])], 0)
    if rows % 16 == 8 and rows > 8:
        return jnp.concatenate([mm(v[: rows - 8], whi, wlo), mm(v[rows - 8 :], whi, wlo)], 0)
    hi, lo = split(v)
    both = jnp.dot(jnp.concatenate([hi, lo], 0), whi, preferred_element_type=F32)
    return both[:rows] + both[rows:] + jnp.dot(hi, wlo, preferred_element_type=F32)


def plus_offset(rows, offset):
    n = rows.shape[0] - rows.shape[0] % HALF
    return jnp.concatenate([rows[:n], rows[n:] + offset], 0)


def whole(halves):
    return jnp.concatenate([halves[0, 0:HALF, :], halves[1, 0:HALF, :], halves[0, HALF:ROWS, :]], 0)


def kernel(
    obs_hbm, mask_hbm, gain_hbm, trans_hbm, scale_hbm, init_hbm, both_out,
    obs, mask, gain, trans, scale, init,
    rf, atf, athi, atlo, hp, hphi, hplo, xt, mk, khi, klo, mv, vo, vhi, vlo, sm, tm, pre, thi, tlo, pc, phi, plo,
    exhi, exlo, eyhi, eylo, nb, nhi, nlo, ret4, frc4, gin, gout, ent, st, fs, fb, sb, wb, vb, eb,
    fh, sh, frecv, srecv,
    in_sem, m_send, m_recv, k_send, k_recv, ks_send, ks_recv, w_send, w_recv, ws_send, ws_recv,
    p_send, p_recv, n_send, n_recv, ns_send, ns_recv, g_send, g_recv, v_send, v_recv,
    of_send, os_send, of_recv, os_recv,
):
    seg, y, c = lax.axis_index("seg"), lax.axis_index("grp"), lax.axis_index("pair")
    x, z = lax.div(seg, ZN), lax.rem(seg, ZN)
    q, r = lax.div(z, CH), lax.rem(z, CH)
    other = 1 - c

    def place(k):
        return jnp.where(
            k < 2,
            jnp.where(k == 0, WORKER[0], WORKER[1]),
            jnp.where(k == 2, WORKER[2], WORKER[3]),
        )

    wz = place(q)
    is_worker = z == wz

    fetches = [
        pltpu.make_async_copy(src, dst, in_sem.at[k])
        for k, (src, dst) in enumerate(
            (
                (mask_hbm, mask), (obs_hbm, obs), (gain_hbm, gain),
                (trans_hbm, trans), (scale_hbm, scale), (init_hbm, init),
            )
        )
    ]
    for fetch in fetches:
        fetch.start()

    def at(xx, yy, zz, cc):
        return {"seg": xx * ZN + zz, "grp": yy, "pair": cc}

    sibling = at(x, y, z, other)

    def copy(src, dst, send, recv, where):
        return pltpu.make_async_remote_copy(
            src_ref=src, dst_ref=dst, send_sem=send, recv_sem=recv,
            device_id=where, device_id_type=pl.DeviceIdType.MESH,
        )

    def arrival(dst, send, recv):
        return copy(dst, dst, send, recv, sibling)

    barrier = pltpu.get_barrier_semaphore()

    def greet(where):
        pl.semaphore_signal(
            barrier, inc=1, device_id=where, device_id_type=pl.DeviceIdType.MESH
        )

    def ring_peer(d):
        return at(x, y, place(lax.rem(q + d, QN)), c)

    def plane_peer(k):
        return at(lax.rem(x + k % XN, XN), lax.rem(y + k // XN, YN), z, c)

    @pl.when(is_worker)
    def _():
        for k in range(1, CH):
            greet(at(x, y, q * CH + lax.rem(r + k, CH), c))
        for k in range(1, QN):
            greet(ring_peer(k))
        for k in range(1, RINGS):
            greet(plane_peer(k))
        greet(sibling)

    @pl.when(jnp.logical_not(is_worker))
    def _():
        greet(at(x, y, wz, c))

    for fetch in fetches[:3]:
        fetch.wait()
    observed = mask[...].astype(F32) * gain[...]
    rf[r, 0:DAYS, :] = 1.0 - observed
    rf[r, DAYS : 2 * DAYS, :] = observed * obs[...]

    @pl.when(jnp.logical_not(is_worker))
    def _():
        pl.semaphore_wait(barrier, 1)
        to_worker = copy(rf.at[r], rf.at[r], m_send, m_recv.at[r], at(x, y, wz, c))
        to_worker.start()
        for fetch in fetches[3:]:
            fetch.wait()
        to_worker.wait_send()
        arrival(frecv, m_send, of_recv).wait_recv()
        both_out[0:DAYS] = frecv[...]
        arrival(srecv, m_send, os_recv).wait_recv()
        both_out[DAYS:] = srecv[...]

    @pl.when(is_worker)
    def _():
        for fetch in fetches[3:]:
            fetch.wait()

        at_full = trans[...].T
        atf[...] = at_full
        athi[...], atlo[...] = split(at_full)

        def advance(chip, first, rows):
            def day(j, rows):
                rows = plus_offset(
                    mm(rows, athi[...], atlo[...]) * rf[chip, pl.ds(j, 1), :],
                    rf[chip, pl.ds(DAYS + j, 1), :],
                )
                xt[chip * DAYS + j] = rows
                return rows

            for j in range(first, DAYS):
                rows = day(j, rows)
            return rows

        def chunk_here(k):
            @pl.when(r != k)
            def _():
                arrival(rf.at[k], m_send, m_recv.at[k]).wait_recv()

        chunk_here(0)
        rows = jnp.concatenate(
            [
                atf[pl.ds(pl.multiple_of(c * HALF, HALF), HALF), :] * rf[0, 0:1, :],
                jnp.broadcast_to(rf[0, DAYS : DAYS + 1, :], (8, M)),
            ],
            0,
        )
        xt[0] = rows
        rows = advance(0, 1, rows)
        for k in range(1, CH):
            chunk_here(k)
            rows = advance(k, 0, rows)
        mk[q, c] = rows

        pl.semaphore_wait(barrier, CH - 1 + QN - 1 + RINGS - 1 + 1)

        def ring_send(buf, send, recv, d):
            return copy(buf.at[q, c], buf.at[q, c], send.at[d], recv.at[q], ring_peer(d))

        def ring_share(buf, send, recv, k):
            return copy(buf.at[k, c], buf.at[k, c], send.at[k], recv.at[k], sibling)

        for d in (2, 1, 3):
            ring_send(mk, k_send, k_recv, d).start()
        ring_share(mk, ks_send, ks_recv, q).start()

        def chunk_share(k):
            return copy(xt.at[k * DAYS - 1], pc.at[k - 1], p_send.at[k - 1], p_recv.at[k - 1], sibling)

        h0 = trans[...] * scale[...]
        hp[...] = h0
        hphi[0], hplo[0] = split(h0)

        weight = 1.0 - scale[...] * jnp.sum(trans[...] * trans[...], axis=0, keepdims=True)

        def back(k, rows):
            return xt[QD - 2 - k] * weight + mm(rows, hphi[0], hplo[0])

        mv[q, c] = lax.fori_loop(0, QD - 1, back, xt[QD - 1] * weight)
        for k in range(1, CH):
            chunk_share(k).start()

        for d in (1, 3, 2):
            k = lax.rem(q + d, QN)
            arrival(mk.at[k, c], k_send.at[d], k_recv.at[k]).wait_recv()
            ring_share(mk, ks_send, ks_recv, k).start()
        for d in (2, 1, 3):
            ring_send(mv, w_send, w_recv, d).start()
        ring_share(mv, ws_send, ws_recv, q).start()
        for k in range(QN):
            ring_share(mk, ks_send, ks_recv, k).wait_recv()
            for half in range(2):
                part = slice(half * HALF, (half + 1) * HALF)
                khi[k, part, :], klo[k, part, :] = split(mk[k, half, 0:HALF, :])
        rows = mk[0, c]
        for k in range(1, QN):
            rows = plus_offset(mm(rows, khi[k], klo[k]), mk[k, 0, HALF : HALF + 1, :])
        nb[x, c] = rows

        def to_peer(d):
            return copy(
                nb.at[x, c], nb.at[x, c], n_send.at[d], n_recv.at[x],
                at(lax.rem(x + d, XN), y, z, c),
            )

        def share(xs):
            return copy(nb.at[xs, c], nb.at[xs, c], ns_send.at[xs], ns_recv.at[xs], sibling)

        for d in (2, 1, 3):
            to_peer(d).start()
        share(x).start()

        def square(k, _):
            h = hp[...]
            h = jnp.dot(h, h, precision=lax.Precision.HIGHEST, preferred_element_type=F32)
            hp[...] = h
            hphi[k], hplo[k] = split(h)
            return 0

        lax.fori_loop(1, POWERS, square, 0)

        def power(k):
            return hphi[k].astype(F32) + hplo[k].astype(F32)

        exhi[0], exlo[0] = hphi[0], hplo[0]
        exhi[1], exlo[1] = split(mm(power(3), hphi[0], hplo[0]))
        exhi[2], exlo[2] = split(mm(power(4), hphi[0], hplo[0]))
        exhi[3], exlo[3] = split(mm(power(4), exhi[1], exlo[1]))
        ret4[...] = jnp.zeros_like(ret4)
        frc4[...] = jnp.zeros_like(frc4)
        for k in range(CH):
            ret4[:, k, :] = rf[k, 0:DAYS, :]
            frc4[:, k, :] = rf[k, DAYS : 2 * DAYS, :]
        for k in range(1, CH):
            arrival(pc.at[k - 1], p_send.at[k - 1], p_recv.at[k - 1]).wait_recv()
            mine, theirs = split(xt[k * DAYS - 1, 0:HALF, :]), split(pc[k - 1, 0:HALF, :])
            own = pl.ds(pl.multiple_of(c * HALF, HALF), HALF)
            far = pl.ds(pl.multiple_of(other * HALF, HALF), HALF)
            phi[k - 1, own, :], plo[k - 1, own, :] = mine
            phi[k - 1, far, :], plo[k - 1, far, :] = theirs
        for d in (1, 3, 2):
            xs = lax.rem(x + d, XN)
            arrival(nb.at[xs, c], n_send.at[d], n_recv.at[xs]).wait_recv()
            share(xs).start()
        for xs in range(XN):
            share(xs).wait_recv()
            for half in range(2):
                part = slice(half * HALF, (half + 1) * HALF)
                nhi[xs, part, :], nlo[xs, part, :] = split(nb[xs, half, 0:HALF, :])

        def smoother_map():
            for d in (1, 3, 2):
                k = lax.rem(q + d, QN)
                arrival(mv.at[k, c], w_send.at[d], w_recv.at[k]).wait_recv()
                ring_share(mv, ws_send, ws_recv, k).start()
            for k in range(QN):
                ring_share(mv, ws_send, ws_recv, k).wait_recv()
            sm[...] = whole(mv[QN - 1])
            for k in (2, 1, 0):

                @pl.when(q == k)
                def _():
                    vhi[1], vlo[1] = split(sm[0:M, :])
                    vo[1] = sm[M : M + 8, :]

                later = mm(sm[...], hphi[5], hplo[5])
                lhi, llo = split(later[:M])
                sm[...] = (
                    plus_offset(mm(whole(mk[k]), lhi, llo), later[M:]) + whole(mv[k])
                )
            vhi[0], vlo[0] = split(sm[0:M, :])
            vo[0] = sm[M : M + 8, :]

        def group_map():
            tm[...] = whole(nb[0])
            for k in range(1, XN):

                @pl.when(x == k)
                def _():
                    pre[...] = tm[...]

                tm[...] = plus_offset(mm(tm[...], nhi[k], nlo[k]), nb[k, 0, HALF : HALF + 1, :])
            thi[0], tlo[0] = split(tm[0:M, :])
            thi[1], tlo[1] = split(pre[0:M, :])

        def to_group():
            return copy(gout, gin, g_send, g_recv, at(x, lax.rem(y + 1, YN), z, c))

        left = QN - 1 - q

        def behind_quads():
            def fold(k, _):
                for bit in range(2):
                    src = (exhi, exlo) if bit == 0 else (eyhi, eylo)

                    @pl.when(lax.rem(lax.div(left, 1 << bit), 2) == 1)
                    def _():
                        whole_map = src[0][k].astype(F32) + src[1][k].astype(F32)
                        eyhi[k], eylo[k] = split(mm(whole_map, hphi[5 + bit], hplo[5 + bit]))

                    if bit == 0:

                        @pl.when(lax.rem(left, 2) == 0)
                        def _():
                            eyhi[k], eylo[k] = exhi[k], exlo[k]

                return 0

            lax.fori_loop(0, CH, fold, 0)

        def expand(vector, xhi, xlo):
            first = jnp.concatenate(
                [mm(vector, xhi[k], xlo[k])[0:1, :] for k in range(CH)]
                + [jnp.zeros((8 - CH, M), F32)],
                0,
            )
            found = first
            for k in range(3):
                found = jnp.concatenate([found, mm(found, hphi[k], hplo[k])], 0)
            for k in range(CH):
                for j in range(DAYS):
                    t = QD - 1 - DAYS * k - j
                    wb[t : t + 1, :] = found[8 * j + k : 8 * j + k + 1, :]

        @pl.when(y == 0)
        def _():
            state = jnp.broadcast_to(init[...], (8, M))
            for k in range(XN):
                ent[k] = state
                state = mm(state, nhi[k], nlo[k]) + nb[k, 0, HALF : HALF + 1, :]
            gout[...] = state
            to_group().start()
            st[0] = ent[x]

        @pl.when(y > 0)
        def _():
            group_map()

        @pl.when(y > 1)
        def _():
            smoother_map()

        @pl.when(y == YN - 1)
        def _():
            behind_quads()

        @pl.when(y > 0)
        def _():
            arrival(gin, g_send, g_recv).wait_recv()
            gout[...] = mm(gin[...], thi[0], tlo[0]) + tm[M : M + 1, :]

            @pl.when(y < YN - 1)
            def _():
                to_group().start()

            st[0] = jnp.where(
                x == 0, gin[...], mm(gin[...], thi[1], tlo[1]) + pre[M : M + 1, :]
            )

        @pl.when(y < 2)
        def _():
            smoother_map()

        v = (mm(st[0], vhi[0], vlo[0]) + vo[0, 0:1, :])[0:1, :]
        boundary = mm(gout[...], athi[...], atlo[...])
        me = y * XN + x
        vb[me] = jnp.concatenate(
            [v[:, :HALF], v[:, HALF:], boundary[0:1, :HALF], boundary[0:5, HALF:]],
            0,
        )

        def to_plane(k):
            return copy(vb.at[me], vb.at[me], v_send.at[k], v_recv.at[me], plane_peer(k))

        plane = (10, 2, 8, 6, 9, 11, 14, 5, 7, 13, 15, 1, 3, 4, 12)
        for k in plane:
            to_plane(k).start()

        for k in range(1, QN):
            st[k] = mm(st[k - 1], khi[k - 1], klo[k - 1]) + mk[k - 1, 0, HALF : HALF + 1, :]
        state = st[q]
        after = mm(st[lax.min(q + 1, QN - 1)], vhi[1], vlo[1]) + vo[1, 0:1, :]
        fs[...] = jnp.zeros_like(fs)
        fs[0:1, :] = state[0:1, :]
        for k in range(1, CH):
            fs[k : k + 1, :] = (
                mm(state, phi[k - 1], plo[k - 1]) + pc[k - 1, HALF : HALF + 1, :]
            )[0:1, :]
        days = fs[...]
        for j in range(DAYS):
            days = mm(days, athi[...], atlo[...]) * ret4[j] + frc4[j]
            for k in range(CH):
                fb[k * DAYS + j : k * DAYS + j + 1, :] = days[k : k + 1, :]

        @pl.when(c == 0)
        def _():
            fh[...] = fb[:, 0:HALF]

        @pl.when(c == 1)
        def _():
            fh[...] = fb[:, HALF:M]

        def out_copy(src, dst, send, recv, k):
            chip = lax.rem(r + k, CH)
            return copy(
                src.at[pl.ds(pl.multiple_of(chip * DAYS, DAYS), DAYS)], dst, send.at[k], recv,
                at(x, y, q * CH + chip, c),
            )

        own_days = pl.ds(pl.multiple_of(r * DAYS, DAYS), DAYS)

        for k in (3, 2, 1):
            out_copy(fh, frecv, of_send, of_recv, k).start()
        both_out[0:DAYS] = fh[own_days, :]

        sb[0:QD, :] = fb[...] * weight
        sb[QD : 2 * QD, :] = jnp.zeros((QD, M), F32)
        for k in range(5):
            sb[0:QD, :] = sb[0:QD, :] + mm(sb[1 << k : (1 << k) + QD, :], hphi[k], hplo[k])

        @pl.when(y < YN - 1)
        def _():
            behind_quads()

        expand(jnp.where(left > 0, after, 0.0), exhi, exlo)
        sb[0:QD, :] = sb[0:QD, :] + wb[...]

        eb[...] = jnp.zeros_like(eb)
        for k in plane:
            src = lax.rem(y + k // XN, YN) * XN + lax.rem(x + k % XN, XN)
            arrival(vb.at[src], v_send.at[k], v_recv.at[src]).wait_recv()
        for half in range(2):
            part = slice(half * HALF, (half + 1) * HALF)
            for k in range(1, RINGS):
                eb[k - 1 : k, part] = vb[k, half : half + 1, :]
            eb[RINGS - 1 : RINGS, part] = vb[RINGS - 1, 2 + half : 3 + half, :]
        for k in range(4):
            eb[0:16, :] = eb[0:16, :] + mm(eb[1 << k : (1 << k) + 16, :], hphi[7 + k], hplo[7 + k])
        behind = jnp.broadcast_to(eb[pl.ds(me, 1), :], (8, M))
        expand(behind, eyhi, eylo)
        total = sb[0:QD, :] + wb[...]

        @pl.when(c == 0)
        def _():
            sh[...] = total[:, 0:HALF]

        @pl.when(c == 1)
        def _():
            sh[...] = total[:, HALF:M]

        for k in (3, 2, 1):
            out_copy(sh, srecv, os_send, os_recv, k).start()
        both_out[DAYS:] = sh[own_days, :]

        for d in range(1, QN):
            ring_send(mk, k_send, k_recv, d).wait_send()
            ring_send(mv, w_send, w_recv, d).wait_send()
            chunk_share(d).wait_send()
        for k in range(QN):
            ring_share(mk, ks_send, ks_recv, k).wait_send()
            ring_share(mv, ws_send, ws_recv, k).wait_send()
        for d in range(1, XN):
            to_peer(d).wait_send()
        for xs in range(XN):
            share(xs).wait_send()

        @pl.when(y < YN - 1)
        def _():
            to_group().wait_send()

        for k in plane:
            to_plane(k).wait_send()
        for k in (3, 2, 1):
            out_copy(fh, frecv, of_send, of_recv, k).wait_send()
            out_copy(sh, srecv, os_send, os_recv, k).wait_send()


def shards(observations, masks, gains, transition, smoother_scale, initial_mean):
    hbm, vmem = pl.BlockSpec(memory_space=pltpu.HBM), pl.BlockSpec(memory_space=pltpu.VMEM)
    dma = pltpu.SemaphoreType.DMA

    def buf(*shape, dtype=F32):
        return pltpu.VMEM(shape, dtype)

    def halves(*shape):
        return [buf(*shape, dtype=BF16), buf(*shape, dtype=BF16)]

    out = jax.ShapeDtypeStruct((2 * DAYS, HALF), F32)
    both = pl.pallas_call(
        kernel,
        out_shape=out,
        in_specs=[hbm] * 6,
        out_specs=vmem,
        scratch_shapes=[
            buf(DAYS, M), buf(DAYS, M, dtype=jnp.int32), buf(1, M), buf(M, M), buf(1, M), buf(1, M),
            buf(CH, 2 * DAYS, M), buf(M, M), *halves(M, M),
            buf(M, M), *halves(POWERS, M, M),
            buf(QD, ROWS, M),
            buf(QN, 2, ROWS, M), *halves(QN, M, M),
            buf(QN, 2, ROWS, M), buf(2, 8, M), *halves(2, M, M),
            buf(M + 8, M), buf(M + 8, M), buf(M + 8, M), *halves(2, M, M),
            buf(CH - 1, ROWS, M), *halves(CH - 1, M, M),
            *halves(CH, M, M), *halves(CH, M, M),
            buf(XN, 2, ROWS, M), *halves(XN, M, M),
            buf(DAYS, 8, M), buf(DAYS, 8, M),
            buf(8, M), buf(8, M), buf(XN, 8, M), buf(QN, 8, M),
            buf(8, M), buf(QD, M), buf(2 * QD, M), buf(QD, M),
            buf(RINGS, 8, HALF), buf(32, M),
            buf(QD, HALF), buf(QD, HALF), buf(DAYS, HALF), buf(DAYS, HALF),
            dma((6,)), dma, dma((CH,)),
            dma((QN,)), dma((QN,)), dma((QN,)), dma((QN,)),
            dma((QN,)), dma((QN,)), dma((QN,)), dma((QN,)),
            dma((CH,)), dma((CH,)),
            dma((XN,)), dma((XN,)), dma((XN,)), dma((XN,)),
            dma, dma, dma((RINGS,)), dma((RINGS,)),
            dma((CH,)), dma((CH,)), dma, dma,
        ],
        compiler_params=pltpu.CompilerParams(
            collective_id=0, has_side_effects=True, vmem_limit_bytes=48 * 2**20
        ),
        name="smoother",
    )(
        observations, masks, gains.reshape(1, M), transition,
        smoother_scale.reshape(1, M), initial_mean.reshape(1, M),
    )
    return both[:DAYS], both[DAYS:]


def solution(mesh):
    return jax.shard_map(
        shards,
        mesh=mesh,
        in_specs=(P(("grp", "seg"), None), P(("grp", "seg"), None), P(), P(), P(), P()),
        out_specs=(P(("grp", "seg"), "pair"), P(("grp", "seg"), "pair")),
        check_vma=False,
    )
```
